256 devices in a mesh: row: 32 (over x, z_hi, core), col: 8 (over z_lo, y).
Axes of the slice: x: 4, y: 4, z: 8 (z_hi: 4, z_lo: 2; z = z_hi * 2 + z_lo), core: 2. Of those that a mesh axis runs over, the one named last changes fastest.
Arguments:
- group: bfloat16 [160, 1024, 128], P('row', 'col'), may hold values from -6 to 6
- pair: bfloat16 [1024, 1024, 128], P('col', 'row'), may hold values from -6 to 6
- mask: int32 [1024], replicated, may hold values from 0 to 1, as said below
- ln_gain: float32 [128], replicated, may hold values from 0.25 to 1.75
- ln_shift: float32 [128], replicated, may hold values from -3 to 3
- w_query: bfloat16 [128, 128], replicated, may hold values from -0.5 to 0.5
- w_key: bfloat16 [128, 128], replicated, may hold values from -0.25 to 0.25
- w_value: bfloat16 [128, 128], replicated, may hold values from -0.5 to 0.5
- w_gate: bfloat16 [128, 128], replicated, may hold values from -0.5 to 0.5
- gate_bias: float32 [128], replicated, may hold values from -4 to 4
- w_bias: bfloat16 [128, 4], replicated, may hold values from -0.1875 to 0.1875
- w_out: bfloat16 [128, 128], replicated, may hold values from -0.5 to 0.5
- cotangent: bfloat16 [160, 1024, 128], P('row', 'col'), may hold values from -6 to 6
Outputs:
- grad_group: bfloat16 [160, 1024, 128], P('row', 'col')
- grad_pair: bfloat16 [1024, 1024, 128], P('col', 'row')
The draws below stay inside these ranges and needn't reach their ends.
Inputs may be any that keep to these rules, and one draw needn't show every extreme that they name: `mask`: the residues form aligned blocks of 8 positions, one padded chain segment each; in every block the real residues (1) come first and the padding (0) after them, and every block has 4 or more real residues.
All inputs are finite; a program needn't handle non-finite values.
Results may differ from the reference program's by a relative error of at most 0.03.
Values may be sent and summed in bfloat16 or wider, within the bound.
No kernel may reach another device: no remote copies, remote signals or barrier semaphores. Data moves between devices by JAX's collectives and lax.ppermute only.
A program may use at most 64 MiB of HBM per device.

```python
import jax
import jax.numpy as jnp
from jax import lax

C = 128
HEADS = 4
HEAD_DIM = 32
N = 1024
I = 160


def draw_mask(key, part):
    key = jax.random.fold_in(key, 7)
    block_count = N // 8
    live_counts = jax.random.randint(key, (block_count,), 4, 9)
    live_counts = live_counts.at[0].set(6)
    positions = jnp.arange(8, dtype=jnp.int32)
    return (positions[None, :] < live_counts[:, None]).reshape(N).astype(jnp.int32)


def block_scale(rng, extent, split, least, largest):
    factor_of, own = 1.0, jax.random.fold_in(rng, 6)
    for position, shards_of in split:
        steps = jnp.exp(jax.random.uniform(jax.random.fold_in(own, position), (shards_of,), jnp.float32, least / len(split), largest / len(split)))
        factor_of = factor_of * jnp.repeat(steps, extent[position] // shards_of).reshape([-1 if axis == position else 1 for axis in range(len(extent))])
    return factor_of


def normal_values(key, shape, scale, limit, split=(), kind=jnp.bfloat16):
    level = block_scale(key, shape, split, -0.22, 0.18) if split else 1.0
    entries = jax.random.normal(key, shape, jnp.float32) * scale * level
    return jnp.minimum(jnp.maximum(entries, -limit), limit).astype(kind)


def setup_inputs(seed: int = 0) -> dict:
    key_list = jax.random.split(jax.random.key(seed), 14)
    return {
        "group": normal_values(key_list[0], (I, N, C), 1.0, 6.0, ((0, 32), (1, 8))),
        "pair": normal_values(key_list[1], (N, N, C), 1.0, 6.0, ((0, 8), (1, 32))),
        "mask": draw_mask(jax.random.fold_in(key_list[13], 71), 0),
        "ln_gain": jnp.clip(1.0 + 0.15 * jax.random.normal(key_list[3], (C,), jnp.float32), 0.25, 1.75),
        "ln_shift": normal_values(key_list[4], (C,), 0.5, 3.0, (), jnp.float32),
        "w_query": normal_values(key_list[5], (C, HEADS * HEAD_DIM), C ** -0.5, 0.5),
        "w_key": normal_values(key_list[6], (C, HEADS * HEAD_DIM), (4 * C) ** -0.5, 0.25),
        "w_value": normal_values(key_list[7], (C, HEADS * HEAD_DIM), C ** -0.5, 0.5),
        "w_gate": normal_values(key_list[8], (C, HEADS * HEAD_DIM), C ** -0.5, 0.5),
        "gate_bias": normal_values(key_list[9], (HEADS * HEAD_DIM,), 1.0, 4.0, (), jnp.float32),
        "w_bias": normal_values(key_list[10], (C, HEADS), (8 * C) ** -0.5, 0.1875),
        "w_out": normal_values(key_list[11], (HEADS * HEAD_DIM, C), (HEADS * HEAD_DIM) ** -0.5, 0.5),
        "cotangent": normal_values(key_list[12], (I, N, C), 1.0, 6.0, ((0, 32), (1, 8))),
    }


epsilon = 1e-05
highest = lax.Precision.HIGHEST

def normalize(values_in):
    widened = values_in.astype(jnp.float32)
    average = lax.optimization_barrier(jnp.mean(widened, axis=-1, keepdims=True))
    centered = widened - average
    variance = lax.optimization_barrier(jnp.mean(centered * centered, axis=-1, keepdims=True))
    reciprocal = lax.rsqrt(variance + epsilon)
    return (centered * reciprocal, reciprocal)

def norm_backward(upstream, normalized, reciprocal, ln_gain):
    scaled = upstream * ln_gain
    first = lax.optimization_barrier(jnp.mean(scaled, axis=-1, keepdims=True))
    second = lax.optimization_barrier(jnp.mean(scaled * normalized, axis=-1, keepdims=True))
    return reciprocal * (scaled - first - normalized * second)

def rounded(values_in):
    return lax.optimization_barrier(values_in.astype(jnp.bfloat16)).astype(jnp.float32)

def wide_dot(left, right):
    return jnp.dot(left, right, precision=highest, preferred_element_type=jnp.float32)

def attention_row(query_row, key_row, value_row, gating_row, upstream_row, bias_wide, live_keys, score_scale):
    query_wide = query_row.astype(jnp.float32)
    key_wide = key_row.astype(jnp.float32)
    value_wide = value_row.astype(jnp.float32)
    scores = jnp.einsum('jhc,khc->hjk', query_wide, key_wide) + bias_wide
    raised = jnp.where(live_keys, jnp.exp(scores), 0.0)
    weights = raised / lax.optimization_barrier(jnp.sum(raised, axis=-1, keepdims=True))
    weights_low = rounded(weights)
    attended = jnp.einsum('hjk,khc->jhc', weights_low, value_wide)
    grad_attended = rounded(upstream_row * gating_row)
    grad_gate_in = upstream_row * attended * gating_row * (1.0 - gating_row)
    row_delta = lax.optimization_barrier(jnp.sum(grad_attended * attended, axis=-1))
    grad_weights = jnp.einsum('jhc,khc->hjk', grad_attended, value_wide)
    grad_scores = weights * (grad_weights - row_delta.T[:, :, None])
    scores_low = rounded(grad_scores)
    grad_queries = jnp.einsum('hjk,khc->jhc', scores_low, key_wide) * score_scale
    grad_keys = jnp.einsum('hjk,jhc->khc', scores_low, query_wide)
    grad_values = jnp.einsum('hjk,jhc->khc', weights_low, grad_attended)
    return (grad_queries, grad_keys, grad_values, grad_gate_in, grad_scores)

def reference(group, pair, mask, ln_gain, ln_shift, w_query, w_key, w_value, w_gate, gate_bias, w_bias, w_out, cotangent):
    head_width = HEADS * HEAD_DIM
    score_scale = HEAD_DIM ** (-0.5)
    normalized, reciprocal = normalize(group)
    normed = (normalized * ln_gain + ln_shift).astype(jnp.bfloat16)
    flattened = normed.reshape(I * N, C)
    shaped = (I, N, HEADS, HEAD_DIM)
    queries = (jnp.dot(flattened, w_query, preferred_element_type=jnp.float32) * score_scale).astype(jnp.bfloat16).reshape(shaped)
    keys = jnp.dot(flattened, w_key, preferred_element_type=jnp.float32).astype(jnp.bfloat16).reshape(shaped)
    values = jnp.dot(flattened, w_value, preferred_element_type=jnp.float32).astype(jnp.bfloat16).reshape(shaped)
    gating = jax.nn.sigmoid(jnp.dot(flattened, w_gate, preferred_element_type=jnp.float32) + gate_bias).reshape(shaped)
    grad_gated = jnp.dot(cotangent.reshape(I * N, C), w_out.T, preferred_element_type=jnp.float32).reshape(shaped)

    def bias_row(pair_slice):
        slice_norm, slice_recip = normalize(pair_slice)
        slice_low = (slice_norm * ln_gain + ln_shift).astype(jnp.bfloat16)
        return jnp.dot(slice_low, w_bias, preferred_element_type=jnp.float32).astype(jnp.bfloat16)
    bias_rows = lax.map(bias_row, pair)
    bias_wide = rounded(jnp.transpose(bias_rows, (2, 0, 1)).astype(jnp.float32))
    live_keys = mask > 0

    def scan_row(partial_value, inputs):
        grad_q, grad_k, grad_v, grad_g, grad_s = attention_row(*inputs, bias_wide, live_keys, score_scale)
        return (partial_value + grad_s, (grad_q, grad_k, grad_v, grad_g))
    grad_bias, gradients = lax.scan(scan_row, jnp.zeros((HEADS, N, N), jnp.float32), (queries, keys, values, gating, grad_gated))
    grad_normed = wide_dot(gradients[0].reshape(I * N, head_width), w_query.astype(jnp.float32).T)
    grad_normed = grad_normed + wide_dot(gradients[1].reshape(I * N, head_width), w_key.astype(jnp.float32).T)
    grad_normed = grad_normed + wide_dot(gradients[2].reshape(I * N, head_width), w_value.astype(jnp.float32).T)
    grad_normed = grad_normed + wide_dot(gradients[3].reshape(I * N, head_width), w_gate.astype(jnp.float32).T)
    grad_group = norm_backward(grad_normed.reshape(I, N, C), normalized, reciprocal, ln_gain).astype(jnp.bfloat16)
    bias_weight = w_bias.astype(jnp.float32)

    def pair_row(inputs):
        pair_slice, grad_slice = inputs
        slice_norm, slice_recip = normalize(pair_slice)
        upstream = wide_dot(grad_slice.T, bias_weight.T)
        return norm_backward(upstream, slice_norm, slice_recip, ln_gain).astype(jnp.bfloat16)
    grad_pair = lax.map(pair_row, (pair, jnp.transpose(grad_bias, (1, 0, 2))))
    return (grad_group, grad_pair)
```

```python
import jax
import jax.numpy as jnp
from jax import lax
from jax.experimental import pallas as pl
from jax.experimental.pallas import tpu as pltpu
from jax.sharding import PartitionSpec as P

HEADS = 4
HEAD_DIM = 32
BLOCK = 128
EPS = 1e-05
SCALE = HEAD_DIM ** (-0.5)
VMEM_LIMIT = 48 * 1024 * 1024

bf16, f32 = jnp.bfloat16, jnp.float32
NT = (((1,), (1,)), ((), ()))
TN = (((0,), (0,)), ((), ()))


def split_high_low(value):
    high = value.astype(bf16)
    return high, (value - high.astype(f32)).astype(bf16)


def bias_kernel(pair_ref, gain_ref, shift_ref, weight_ref, out_ref, normed, heads):
    gain, shift = gain_ref[...], shift_ref[...]
    weight_t = jnp.concatenate(
        [weight_ref[...].astype(f32), jnp.zeros((BLOCK, BLOCK - HEADS), f32)], axis=1
    ).T[:16].astype(bf16)

    def rows(step, carry):
        x = pair_ref[pl.ds(step * 16, 16)].astype(f32).reshape(512, BLOCK)
        centered = x - jnp.mean(x, axis=-1, keepdims=True)
        reciprocal = lax.rsqrt(jnp.mean(centered * centered, axis=-1, keepdims=True) + EPS)
        low = (centered * reciprocal * gain + shift).astype(bf16).astype(f32)
        normed[pl.ds(pl.multiple_of(step * 512, 512), 512), :] = low
        return carry

    lax.fori_loop(0, 8, rows, 0)

    for k in range(32):
        block = normed[pl.ds(k, BLOCK, stride=32), :].astype(bf16)
        product = lax.dot_general(weight_t, block, NT, preferred_element_type=f32)
        for h in range(HEADS):
            heads[h, k : k + 1, :] = product[h : h + 1]
    for zh in range(4):
        out_ref[zh] = heads[...].astype(bf16)


def bias_call(pair, gain, shift, weight):
    return pl.pallas_call(
        bias_kernel,
        out_shape=jax.ShapeDtypeStruct((4, HEADS, 32, BLOCK), bf16),
        scratch_shapes=[pltpu.VMEM((4096, BLOCK), f32), pltpu.VMEM((HEADS, 32, BLOCK), f32)],
        compiler_params=pltpu.CompilerParams(vmem_limit_bytes=VMEM_LIMIT),
        cost_estimate=pl.CostEstimate(
            flops=20_000_000, bytes_accessed=1_200_000, transcendentals=4096
        ),
        name="pair_bias",
    )(pair, gain, shift, weight)


def project_kernel(
    group_ref, cot_ref, gain_ref, shift_ref, wq_ref, wk_ref, wv_ref, wg_ref, gb_ref, wo_ref,
    key_value, query_up, coef,
):
    gain, shift = gain_ref[...], shift_ref[...]
    turned = [w[...].astype(f32).T.astype(bf16) for w in (wq_ref, wk_ref, wv_ref, wg_ref)]
    gate_bias = jnp.broadcast_to(gb_ref[...], (BLOCK, BLOCK)).T
    rows = group_ref.shape[0]
    for i in range(rows):
        x = group_ref[i].astype(f32)
        centered = x - jnp.mean(x, axis=-1, keepdims=True)
        reciprocal = lax.rsqrt(jnp.mean(centered * centered, axis=-1, keepdims=True) + EPS)
        normed = (centered * reciprocal * gain + shift).astype(bf16)
        dots = [lax.dot_general(w, normed, NT, preferred_element_type=f32) for w in turned]
        gating = jax.nn.sigmoid(dots[3] + gate_bias)
        gated = lax.dot_general(wo_ref[...], cot_ref[i], NT, preferred_element_type=f32)
        upstream = gated * gating
        coef[i] = upstream * (1.0 - gating)
        for n, value in enumerate((dots[1], dots[2], dots[0] * SCALE, upstream)):
            value = value.astype(bf16).reshape(HEADS, HEAD_DIM, BLOCK)
            for h in range(HEADS):
                if n < 2:
                    key_value[0, h, n, i] = value[h]
                    key_value[1, h, n, i] = value[h]
                else:
                    query_up[h, n - 2, i] = value[h]


def project_call(group, cotangent, gain, shift, wq, wk, wv, wg, gb, wo):
    rows = group.shape[0]
    return pl.pallas_call(
        project_kernel,
        out_shape=(
            jax.ShapeDtypeStruct((2, HEADS, 2, rows, HEAD_DIM, BLOCK), bf16),
            jax.ShapeDtypeStruct((HEADS, 2, rows, HEAD_DIM, BLOCK), bf16),
            jax.ShapeDtypeStruct((rows, BLOCK, BLOCK), f32),
        ),
        compiler_params=pltpu.CompilerParams(vmem_limit_bytes=VMEM_LIMIT),
        cost_estimate=pl.CostEstimate(
            flops=110_000_000, bytes_accessed=2_000_000, transcendentals=100_000
        ),
        name="project",
    )(group, cotangent, gain, shift, wq, wk, wv, wg, gb, wo)


def attention_kernel(
    mask_ref, bias_own, bias_other, key_value, query_up, out_kv, out_q, keep, send,
    bias, grad, key_t, value_t, key_s, value_s,
):
    core = lax.axis_index("core")
    keys, queries = bias.shape
    rows = query_up.shape[2]

    for source, c in ((bias_own, core), (bias_other, 1 - core)):
        for n in range(16):
            at = pl.ds(pl.multiple_of(n * 64 + c * 32, 32), 32)
            for y in range(4):
                bias[at, y * BLOCK : (y + 1) * BLOCK] = source[n // 4, n % 4, y].astype(f32)
    for blk in range(keys // BLOCK):
        at = slice(blk * BLOCK, (blk + 1) * BLOCK)
        live = jnp.broadcast_to(mask_ref[blk : blk + 1, :].astype(f32), (BLOCK, BLOCK)).T
        for y in range(4):
            lanes = slice(y * BLOCK, (y + 1) * BLOCK)
            bias[at, lanes] = jnp.where(live > 0.0, bias[at, lanes], -jnp.inf)
        for i in range(rows):
            k, v = key_value[blk // 4, blk % 4, 0, i], key_value[blk // 4, blk % 4, 1, i]
            key_t[i, :, at] = k
            value_t[i, :, at] = v
            key_s[i, at, :] = k.astype(f32).T.astype(bf16)
            value_s[i, at, :] = v.astype(f32).T.astype(bf16)
    grad[...] = jnp.zeros_like(grad)

    width = 256

    def row(i, carry):
        grad_key = jnp.zeros((keys, HEAD_DIM), f32)
        grad_value = jnp.zeros((keys, HEAD_DIM), f32)
        for part in range(queries // width):
            lanes = slice(part * width, (part + 1) * width)
            blocks = range(part * (width // BLOCK), (part + 1) * (width // BLOCK))
            q = jnp.concatenate([query_up[n, 0, i] for n in blocks], axis=1)
            g = jnp.concatenate([query_up[n, 1, i] for n in blocks], axis=1)
            scores = jnp.dot(key_s[i], q, preferred_element_type=f32) + bias[:, lanes]
            raised = jnp.exp(scores)
            weights = raised * (1.0 / jnp.sum(raised, axis=0, keepdims=True))
            low = weights.astype(bf16)
            attended = jnp.dot(value_t[i], low, preferred_element_type=f32)
            delta = jnp.sum(g.astype(f32) * attended, axis=0, keepdims=True)
            grad_weights = jnp.dot(value_s[i], g, preferred_element_type=f32)
            grad_scores = weights * (grad_weights - delta)
            grad[:, lanes] += grad_scores
            scores_low = grad_scores.astype(bf16)
            grad_query = jnp.dot(key_t[i], scores_low, preferred_element_type=f32) * SCALE
            grad_key += lax.dot_general(scores_low, q, NT, preferred_element_type=f32)
            grad_value += lax.dot_general(low, g, NT, preferred_element_type=f32)
            for n, block in enumerate(blocks):
                at = slice(n * BLOCK, (n + 1) * BLOCK)
                out_q[block, 0, i] = grad_query[:, at].astype(bf16)
                out_q[block, 1, i] = attended[:, at].astype(bf16)
        both = jnp.concatenate([grad_key, grad_value], axis=1).T.astype(bf16)
        for blk in range(keys // BLOCK):
            at = slice(blk * BLOCK, (blk + 1) * BLOCK)
            out_kv[blk // 4, blk % 4, 0, i] = both[:HEAD_DIM, at]
            out_kv[blk // 4, blk % 4, 1, i] = both[HEAD_DIM:, at]
        return carry

    lax.fori_loop(0, rows, row, 0)

    for out, c in ((keep, core), (send, 1 - core)):
        for n in range(16):
            at = pl.ds(pl.multiple_of(n * 64 + c * 32, 32), 32)
            for y in range(4):
                piece = grad[at, y * BLOCK : (y + 1) * BLOCK]
                out[n // 4, n % 4, y] = piece.astype(out.dtype)


def attention_call(mask, bias_own, bias_other, key_value, query_up):
    rows = query_up.shape[2]
    keys = mask.shape[0] * mask.shape[1]
    queries = keys // 2
    return pl.pallas_call(
        attention_kernel,
        out_shape=(
            jax.ShapeDtypeStruct(key_value.shape, bf16),
            jax.ShapeDtypeStruct(query_up.shape, bf16),
            jax.ShapeDtypeStruct(bias_own.shape, f32),
            jax.ShapeDtypeStruct(bias_own.shape, bf16),
        ),
        scratch_shapes=[
            pltpu.VMEM((keys, queries), f32),
            pltpu.VMEM((keys, queries), f32),
            pltpu.VMEM((rows, HEAD_DIM, keys), bf16),
            pltpu.VMEM((rows, HEAD_DIM, keys), bf16),
            pltpu.VMEM((rows, keys, HEAD_DIM), bf16),
            pltpu.VMEM((rows, keys, HEAD_DIM), bf16),
        ],
        compiler_params=pltpu.CompilerParams(vmem_limit_bytes=VMEM_LIMIT),
        cost_estimate=pl.CostEstimate(
            flops=8_000_000_000, bytes_accessed=6_000_000, transcendentals=2_700_000
        ),
        name="attention",
    )(mask, bias_own, bias_other, key_value, query_up)


def add_two_kernel(keep, came, out):
    out[...] = (keep[...] + came[...].astype(f32)).astype(bf16)


def add_four_kernel(came, out):
    wide = [came[n].astype(f32) for n in range(4)]
    out[...] = ((wide[0] + wide[1]) + (wide[2] + wide[3])).astype(bf16)


def add_call(kernel, shape, *values):
    return pl.pallas_call(
        kernel,
        out_shape=jax.ShapeDtypeStruct(shape, bf16),
        compiler_params=pltpu.CompilerParams(vmem_limit_bytes=VMEM_LIMIT),
        name="add_bias_gradient",
    )(*values)


def group_kernel(
    group_ref, gain_ref, wq_ref, wk_ref, wv_ref, wg_ref, coef, grad_kv, grad_q, out_ref
):
    gain = gain_ref[...]
    wq, wk, wv, wg = wq_ref[...], wk_ref[...], wv_ref[...], wg_ref[...]
    weights = jnp.concatenate([wq, wk, wk, wv, wv, wg, wg], axis=1)
    for i in range(group_ref.shape[0]):
        parts = [[] for _ in range(7)]
        for h in range(HEADS):
            gate = coef[i, h * HEAD_DIM : (h + 1) * HEAD_DIM, :] * grad_q[h, 1, i].astype(f32)
            high, low = split_high_low(gate)
            pieces = (
                grad_q[h, 0, i],
                grad_kv[0, h, 0, i], grad_kv[1, h, 0, i],
                grad_kv[0, h, 1, i], grad_kv[1, h, 1, i],
                high, low,
            )
            for part, piece in zip(parts, pieces):
                part.append(piece)
        stacked = jnp.concatenate(sum(parts, []), axis=0)
        upstream = jnp.dot(weights, stacked, preferred_element_type=f32).T
        x = group_ref[i].astype(f32)
        centered = x - jnp.mean(x, axis=-1, keepdims=True)
        reciprocal = lax.rsqrt(jnp.mean(centered * centered, axis=-1, keepdims=True) + EPS)
        normalized = centered * reciprocal
        scaled = upstream * gain
        first = jnp.mean(scaled, axis=-1, keepdims=True)
        second = jnp.mean(scaled * normalized, axis=-1, keepdims=True)
        out_ref[i] = (reciprocal * (scaled - first - normalized * second)).astype(bf16)


def group_call(group, gain, wq, wk, wv, wg, coef, grad_kv, grad_q):
    return pl.pallas_call(
        group_kernel,
        out_shape=jax.ShapeDtypeStruct(group.shape, bf16),
        compiler_params=pltpu.CompilerParams(vmem_limit_bytes=VMEM_LIMIT),
        cost_estimate=pl.CostEstimate(
            flops=160_000_000, bytes_accessed=2_000_000, transcendentals=1000
        ),
        name="group_backward",
    )(group, gain, wq, wk, wv, wg, coef, grad_kv, grad_q)


def pair_kernel(pair_ref, gain_ref, weight_ref, came, out_ref, xhat, recip, grad, db):
    weight = jnp.concatenate(
        [weight_ref[...].astype(f32), jnp.zeros((BLOCK, BLOCK - HEADS), f32)], axis=1
    ).T[:8] * gain_ref[...]
    high, low = split_high_low(weight)
    weights = jnp.concatenate([high, high, low, jnp.zeros((8, BLOCK), bf16)], axis=0)
    db[...] = jnp.zeros_like(db)
    for h in range(HEADS):
        wide = [came[zh, h].astype(f32) for zh in range(4)]
        value = (wide[0] + wide[1]) + (wide[2] + wide[3])
        for k in range(32):
            db[k, h : h + 1, :] = value[k : k + 1]

    def rows(step, carry):
        x = pair_ref[pl.ds(step * 16, 16)].astype(f32).reshape(512, BLOCK)
        centered = x - jnp.mean(x, axis=-1, keepdims=True)
        reciprocal = lax.rsqrt(jnp.mean(centered * centered, axis=-1, keepdims=True) + EPS)
        at = pl.ds(pl.multiple_of(step * 512, 512), 512)
        xhat[at, :] = centered * reciprocal
        recip[at, :] = jnp.broadcast_to(reciprocal, (512, BLOCK))
        return carry

    lax.fori_loop(0, 8, rows, 0)
    for k in range(32):
        db_high, db_low = split_high_low(db[k])
        left = jnp.concatenate([db_high, db_low, db_high, jnp.zeros((8, BLOCK), bf16)], axis=0)
        scaled = lax.dot_general(left, weights, TN, preferred_element_type=f32)
        at = pl.ds(k, BLOCK, stride=32)
        normalized = xhat[at, :]
        first = jnp.mean(scaled, axis=-1, keepdims=True)
        second = jnp.mean(scaled * normalized, axis=-1, keepdims=True)
        grad[at, :] = recip[at, :] * (scaled - first - normalized * second)

    def store(step, carry):
        at = pl.ds(pl.multiple_of(step * 512, 512), 512)
        out_ref[pl.ds(step * 16, 16)] = grad[at, :].astype(bf16).reshape(16, 32, BLOCK)
        return carry

    lax.fori_loop(0, 8, store, 0)


def pair_call(pair, gain, weight, came):
    big = pltpu.VMEM((4096, BLOCK), f32)
    return pl.pallas_call(
        pair_kernel,
        out_shape=jax.ShapeDtypeStruct(pair.shape, bf16),
        scratch_shapes=[big, big, big, pltpu.VMEM((32, 8, BLOCK), f32)],
        compiler_params=pltpu.CompilerParams(vmem_limit_bytes=VMEM_LIMIT),
        cost_estimate=pl.CostEstimate(
            flops=60_000_000, bytes_accessed=2_200_000, transcendentals=4096
        ),
        name="pair_backward",
    )(pair, gain, weight, came)


def exchange(value, axes):
    return lax.all_to_all(value, axes, split_axis=0, concat_axis=0, tiled=True)


def other_core(value):
    return lax.ppermute(value, "core", [(0, 1), (1, 0)])


def per_device(
    group, pair, mask, ln_gain, ln_shift, w_query, w_key, w_value, w_gate, gate_bias, w_bias,
    w_out, cotangent,
):
    gain, shift = ln_gain.reshape(1, BLOCK), ln_shift.reshape(1, BLOCK)
    pieces = bias_call(pair, gain, shift, w_bias)
    near = exchange(pieces.reshape(16, 32, BLOCK), ("zh", "y")).reshape(1, 4, 4, 32, BLOCK)
    plane = exchange(jnp.broadcast_to(near, (4, 4, 4, 32, BLOCK)), "x")
    other = other_core(plane)

    key_value, query_up, coef = project_call(
        group, cotangent, gain, shift, w_query, w_key, w_value, w_gate,
        gate_bias.reshape(1, BLOCK), w_out,
    )
    kv_shape = key_value.shape
    flat = (8,) + kv_shape[2:]
    key_value = exchange(key_value.reshape(flat), ("z", "y")).reshape(kv_shape)
    query_up = exchange(query_up, "y")

    grad_kv, grad_q, keep, send = attention_call(
        mask.reshape(-1, BLOCK), plane, other, key_value, query_up
    )

    both = add_call(add_two_kernel, keep.shape, keep, other_core(send))
    line = add_call(add_four_kernel, keep.shape[1:], exchange(both, "x"))
    came = exchange(line.reshape(16, 32, BLOCK), ("zh", "y")).reshape(line.shape)

    grad_kv = exchange(grad_kv.reshape(flat), ("z", "y")).reshape(kv_shape)
    grad_q = exchange(grad_q, "y")
    grad_group = group_call(group, gain, w_query, w_key, w_value, w_gate, coef, grad_kv, grad_q)
    grad_pair = pair_call(pair, gain, w_bias, came)
    return (grad_group, grad_pair)


def solution(mesh):
    fine = jax.sharding.Mesh(mesh.devices.reshape(4, 4, 2, 2, 4), ("x", "zh", "core", "z", "y"))
    row, col = ("x", "zh", "core"), ("z", "y")
    placed = (
        P(row, col, None),
        P(col, row, None),
        P(), P(), P(), P(), P(), P(), P(), P(), P(), P(),
        P(row, col, None),
    )
    return jax.shard_map(
        per_device,
        mesh=fine,
        in_specs=placed,
        out_specs=(P(row, col, None), P(col, row, None)),
        check_vma=False,
    )
```

```python
import jax
import jax.numpy as jnp
from jax import lax
from jax.experimental import pallas as pl
from jax.experimental.pallas import tpu as pltpu
from jax.sharding import PartitionSpec as P

HEADS = 4
HEAD_DIM = 32
BLOCK = 128
EPS = 1e-05
SCALE = HEAD_DIM ** (-0.5)
VMEM_LIMIT = 48 * 1024 * 1024

bf16, f32 = jnp.bfloat16, jnp.float32
NT = (((1,), (1,)), ((), ()))
TN = (((0,), (0,)), ((), ()))


def place():
    return tuple(lax.axis_index(name) for name in ("x", "zh", "core", "z", "y"))


def split_high_low(value):
    high = value.astype(bf16)
    return high, (value - high.astype(f32)).astype(bf16)


def front_kernel(
    group_ref, cot_ref, pair_ref, gain_ref, shift_ref, wq_ref, wk_ref, wv_ref, wg_ref, gb_ref,
    wo_ref, wb_ref, s0, s1, s2, s3, coef, normed, heads, parts,
):
    _, _, _, _, y = place()
    gain, shift = gain_ref[...], shift_ref[...]
    turned = [w[...].astype(f32).T.astype(bf16) for w in (wq_ref, wk_ref, wv_ref, wg_ref)]
    gate_bias = jnp.broadcast_to(gb_ref[...], (BLOCK, BLOCK)).T
    rows = group_ref.shape[0]
    for i in range(rows):
        x = group_ref[i].astype(f32)
        centered = x - jnp.mean(x, axis=-1, keepdims=True)
        reciprocal = lax.rsqrt(jnp.mean(centered * centered, axis=-1, keepdims=True) + EPS)
        low = (centered * reciprocal * gain + shift).astype(bf16)
        dots = [lax.dot_general(w, low, NT, preferred_element_type=f32) for w in turned]
        gating = jax.nn.sigmoid(dots[3] + gate_bias)
        gated = lax.dot_general(wo_ref[...], cot_ref[i], NT, preferred_element_type=f32)
        upstream = gated * gating
        coef[i] = upstream * (1.0 - gating)
        for n, value in enumerate((dots[1], dots[2], dots[0] * SCALE, upstream)):
            value = value.astype(bf16).reshape(HEADS, HEAD_DIM, BLOCK)
            for h in range(HEADS):
                parts[h, n * rows + i] = value[h]

    weight_t = jnp.concatenate(
        [wb_ref[...].astype(f32), jnp.zeros((BLOCK, BLOCK - HEADS), f32)], axis=1
    ).T[:16].astype(bf16)

    def norm_rows(step, carry):
        x = pair_ref[pl.ds(step * 16, 16)].astype(f32).reshape(512, BLOCK)
        centered = x - jnp.mean(x, axis=-1, keepdims=True)
        reciprocal = lax.rsqrt(jnp.mean(centered * centered, axis=-1, keepdims=True) + EPS)
        low = (centered * reciprocal * gain + shift).astype(bf16).astype(f32)
        normed[pl.ds(pl.multiple_of(step * 512, 512), 512), :] = low
        return carry

    lax.fori_loop(0, 8, norm_rows, 0)

    for k in range(32):
        block = normed[pl.ds(k, BLOCK, stride=32), :].astype(bf16)
        product = lax.dot_general(weight_t, block, NT, preferred_element_type=f32)
        for h in range(HEADS):
            heads[h, k : k + 1, :] = product[h : h + 1]
    for h in range(HEADS):
        parts[h, 4 * rows] = heads[h].astype(bf16)
    for step, out in enumerate((s0, s1, s2, s3)):
        out[...] = parts[lax.rem(y + step, 4)]


def front_call(group, cotangent, pair, *small):
    rows = group.shape[0]
    sent = jax.ShapeDtypeStruct((4 * rows + 1, HEAD_DIM, BLOCK), bf16)
    return pl.pallas_call(
        front_kernel,
        out_shape=(sent,) * 4 + (jax.ShapeDtypeStruct((rows, BLOCK, BLOCK), f32),),
        scratch_shapes=[
            pltpu.VMEM((4096, BLOCK), f32),
            pltpu.VMEM((HEADS, 32, BLOCK), f32),
            pltpu.VMEM((HEADS, 4 * rows + 1, HEAD_DIM, BLOCK), bf16),
        ],
        compiler_params=pltpu.CompilerParams(vmem_limit_bytes=VMEM_LIMIT),
        cost_estimate=pl.CostEstimate(
            flops=130_000_000, bytes_accessed=3_000_000, transcendentals=100_000
        ),
        name="front",
    )(group, cotangent, pair, *small)


def attention_kernel(
    mask_ref, bias_own, bias_other, s0, s1, s2, s3, kv_other,
    out_own, out_other, out_q, keep, send,
    bias, grad, key_t, value_t, key_s, value_s, query_t, up_t, key_out,
):
    x, zh, core, z, y = place()
    keys, queries = bias.shape
    rows = key_t.shape[0]

    for blk in range(keys // BLOCK):
        live = jnp.broadcast_to(mask_ref[blk : blk + 1, :].astype(f32), (BLOCK, BLOCK)).T
        bias[blk * BLOCK : (blk + 1) * BLOCK, :] = jnp.concatenate([live] * (queries // BLOCK), 1)
    for source, c in ((bias_own, core), (bias_other, 1 - core)):
        for dx in range(4):
            for dz in range(4):
                r = lax.rem(x - dx + 4, 4) * 8 + lax.rem(zh - dz + 4, 4) * 2 + c
                at = pl.ds(pl.multiple_of(r * 32, 32), 32)
                for dy in range(4):
                    lanes = slice(dy * BLOCK, (dy + 1) * BLOCK)
                    bias[at, lanes] = jnp.where(
                        bias[at, lanes] > 0.0, source[dx, dz, dy].astype(f32), -jnp.inf
                    )
    grad[...] = jnp.zeros_like(grad)

    for step, own in enumerate((s0, s1, s2, s3)):
        yy = lax.rem(y - step + 4, 4)
        for source, c in ((own, z * 4 + yy), (kv_other.at[step], (1 - z) * 4 + yy)):
            at = pl.ds(pl.multiple_of(c * BLOCK, BLOCK), BLOCK)
            for i in range(rows):
                k, v = source[i], source[rows + i]
                key_t[i, :, at] = k
                value_t[i, :, at] = v
                key_s[i, at, :] = k.astype(f32).T.astype(bf16)
                value_s[i, at, :] = v.astype(f32).T.astype(bf16)
        for i in range(rows):
            query_t[i, :, step * BLOCK : (step + 1) * BLOCK] = own[2 * rows + i]
            up_t[i, :, step * BLOCK : (step + 1) * BLOCK] = own[3 * rows + i]

    width = 256

    def row(i, carry):
        grad_key = jnp.zeros((keys, HEAD_DIM), f32)
        grad_value = jnp.zeros((keys, HEAD_DIM), f32)
        for part in range(queries // width):
            lanes = slice(part * width, (part + 1) * width)
            q, g = query_t[i, :, lanes], up_t[i, :, lanes]
            scores = jnp.dot(key_s[i], q, preferred_element_type=f32) + bias[:, lanes]
            raised = jnp.exp(scores)
            weights = raised * (1.0 / jnp.sum(raised, axis=0, keepdims=True))
            low = weights.astype(bf16)
            attended = jnp.dot(value_t[i], low, preferred_element_type=f32)
            delta = jnp.sum(g.astype(f32) * attended, axis=0, keepdims=True)
            grad_weights = jnp.dot(value_s[i], g, preferred_element_type=f32)
            grad_scores = weights * (grad_weights - delta)
            grad[:, lanes] += grad_scores
            scores_low = grad_scores.astype(bf16)
            grad_query = jnp.dot(key_t[i], scores_low, preferred_element_type=f32) * SCALE
            grad_key += lax.dot_general(scores_low, q, NT, preferred_element_type=f32)
            grad_value += lax.dot_general(low, g, NT, preferred_element_type=f32)
            for n in range(width // BLOCK):
                block, at = part * (width // BLOCK) + n, slice(n * BLOCK, (n + 1) * BLOCK)
                out_q[block, i] = grad_query[:, at].astype(bf16)
                out_q[block, rows + i] = attended[:, at].astype(bf16)
        both = jnp.concatenate([grad_key, grad_value], axis=1).T.astype(bf16)
        key_out[i, 0] = both[:HEAD_DIM]
        key_out[i, 1] = both[HEAD_DIM:]
        return carry

    lax.fori_loop(0, rows, row, 0)

    for step in range(4):
        yy = lax.rem(y - step + 4, 4)
        for out, c in ((out_own, z * 4 + yy), (out_other, (1 - z) * 4 + yy)):
            at = pl.ds(pl.multiple_of(c * BLOCK, BLOCK), BLOCK)
            for i in range(rows):
                out[step, i] = key_out[i, 0, :, at]
                out[step, rows + i] = key_out[i, 1, :, at]
    for out, c in ((keep, core), (send, 1 - core)):
        for dx in range(4):
            for dz in range(4):
                r = lax.rem(x - dx + 4, 4) * 8 + lax.rem(zh - dz + 4, 4) * 2 + c
                at = pl.ds(pl.multiple_of(r * 32, 32), 32)
                for dy in range(4):
                    out[dx, dz, dy] = grad[at, dy * BLOCK : (dy + 1) * BLOCK].astype(out.dtype)


def attention_call(mask, bias_own, bias_other, pieces, kv_other):
    rows = kv_other.shape[1] // 2
    keys = mask.shape[0] * mask.shape[1]
    queries = keys // 2
    part = jax.ShapeDtypeStruct(kv_other.shape, bf16)
    return pl.pallas_call(
        attention_kernel,
        out_shape=(
            part, part, part,
            jax.ShapeDtypeStruct(bias_own.shape, f32),
            jax.ShapeDtypeStruct(bias_own.shape, bf16),
        ),
        scratch_shapes=[
            pltpu.VMEM((keys, queries), f32),
            pltpu.VMEM((keys, queries), f32),
            pltpu.VMEM((rows, HEAD_DIM, keys), bf16),
            pltpu.VMEM((rows, HEAD_DIM, keys), bf16),
            pltpu.VMEM((rows, keys, HEAD_DIM), bf16),
            pltpu.VMEM((rows, keys, HEAD_DIM), bf16),
            pltpu.VMEM((rows, HEAD_DIM, queries), bf16),
            pltpu.VMEM((rows, HEAD_DIM, queries), bf16),
            pltpu.VMEM((rows, 2, HEAD_DIM, keys), bf16),
        ],
        compiler_params=pltpu.CompilerParams(vmem_limit_bytes=VMEM_LIMIT),
        cost_estimate=pl.CostEstimate(
            flops=8_000_000_000, bytes_accessed=6_000_000, transcendentals=2_700_000
        ),
        name="attention",
    )(mask, bias_own, bias_other, *pieces, kv_other)


def add_core_kernel(keep, came, k0, s1, s2, s3):
    for n, out in enumerate((k0, s1, s2, s3)):
        out[...] = (keep[n] + came[n].astype(f32)).astype(out.dtype)


def add_core(keep, came):
    shape = keep.shape[1:]
    return pl.pallas_call(
        add_core_kernel,
        out_shape=(jax.ShapeDtypeStruct(shape, f32),) + (jax.ShapeDtypeStruct(shape, bf16),) * 3,
        compiler_params=pltpu.CompilerParams(vmem_limit_bytes=VMEM_LIMIT),
        name="add_core",
    )(keep, came)


def add_four_kernel(keep, c1, c2, c3, k0, s1, s2, s3):
    for n, out in enumerate((k0, s1, s2, s3)):
        total = keep[n] + c1[n].astype(f32) + c2[n].astype(f32) + c3[n].astype(f32)
        out[...] = total.astype(out.dtype)


def add_four(keep, c1, c2, c3):
    shape = keep.shape[1:]
    return pl.pallas_call(
        add_four_kernel,
        out_shape=(jax.ShapeDtypeStruct(shape, f32),) + (jax.ShapeDtypeStruct(shape, bf16),) * 3,
        compiler_params=pltpu.CompilerParams(vmem_limit_bytes=VMEM_LIMIT),
        name="add_four",
    )(keep, c1, c2, c3)


def pack_kernel(keep, c1, c2, c3, own, came, query, t0, t1, t2, t3):
    half = own.shape[1]
    for n, out in enumerate((t0, t1, t2, t3)):
        out[:half] = (own[n].astype(f32) + came[n].astype(f32)).astype(bf16)
        out[half : 2 * half] = query[n]
        total = keep[n] + c1[n].astype(f32) + c2[n].astype(f32) + c3[n].astype(f32)
        out[2 * half] = total.astype(bf16)


def pack_call(keep, c1, c2, c3, own, came, query):
    half, *tile = own.shape[1:]
    return pl.pallas_call(
        pack_kernel,
        out_shape=(jax.ShapeDtypeStruct((2 * half + 1, *tile), bf16),) * 4,
        compiler_params=pltpu.CompilerParams(vmem_limit_bytes=VMEM_LIMIT),
        name="pack",
    )(keep, c1, c2, c3, own, came, query)


def group_kernel(
    group_ref, gain_ref, wq_ref, wk_ref, wv_ref, wg_ref, coef,
    t0, t1, t2, t3, out_ref,
):
    _, _, _, _, y = place()
    gain = gain_ref[...]
    turn = lax.rem(4 - y, 4) * HEAD_DIM
    wq, wk, wv, wg = (
        pltpu.roll(w[...].astype(f32), turn, 1).astype(bf16)
        for w in (wq_ref, wk_ref, wv_ref, wg_ref)
    )
    weights = jnp.concatenate([wk, wv, wq, wg, wg], axis=1)
    rows = group_ref.shape[0]
    for i in range(rows):
        parts = [[] for _ in range(5)]
        for step, t in enumerate((t0, t1, t2, t3)):
            h = lax.rem(y + step, 4)
            at = pl.multiple_of(h * HEAD_DIM, HEAD_DIM)
            gate = coef[i, pl.ds(at, HEAD_DIM), :] * t[3 * rows + i].astype(f32)
            high, low = split_high_low(gate)
            pieces = (t[i], t[rows + i], t[2 * rows + i], high, low)
            for part, piece in zip(parts, pieces):
                part.append(piece)
        stacked = jnp.concatenate(sum(parts, []), axis=0)
        upstream = jnp.dot(weights, stacked, preferred_element_type=f32).T
        x = group_ref[i].astype(f32)
        centered = x - jnp.mean(x, axis=-1, keepdims=True)
        reciprocal = lax.rsqrt(jnp.mean(centered * centered, axis=-1, keepdims=True) + EPS)
        normalized = centered * reciprocal
        scaled = upstream * gain
        first = jnp.mean(scaled, axis=-1, keepdims=True)
        second = jnp.mean(scaled * normalized, axis=-1, keepdims=True)
        out_ref[i] = (reciprocal * (scaled - first - normalized * second)).astype(bf16)


def group_call(group, gain, wq, wk, wv, wg, coef, pieces):
    return pl.pallas_call(
        group_kernel,
        out_shape=jax.ShapeDtypeStruct(group.shape, bf16),
        compiler_params=pltpu.CompilerParams(vmem_limit_bytes=VMEM_LIMIT),
        cost_estimate=pl.CostEstimate(
            flops=160_000_000, bytes_accessed=2_000_000, transcendentals=1000
        ),
        name="group_backward",
    )(group, gain, wq, wk, wv, wg, coef, *pieces)


def pair_kernel(pair_ref, gain_ref, weight_ref, t0, t1, t2, t3, out_ref, grad, db):
    _, _, _, _, y = place()
    weight = jnp.concatenate(
        [weight_ref[...].astype(f32), jnp.zeros((BLOCK, BLOCK - HEADS), f32)], axis=1
    ).T[:8] * gain_ref[...]
    weight = weight - jnp.mean(weight, axis=-1, keepdims=True)
    high, low = split_high_low(weight)
    weights = jnp.concatenate([high, high, low, jnp.zeros((8, BLOCK), bf16)], axis=0)
    db[...] = jnp.zeros_like(db)
    last = t0.shape[0] - 1
    for step, t in enumerate((t0, t1, t2, t3)):
        h = lax.rem(y + step, 4)
        value = t[last].astype(f32)
        for k in range(32):
            db[k, pl.ds(h, 1), :] = value[k : k + 1]

    for k in range(32):
        db_high, db_low = split_high_low(db[k])
        left = jnp.concatenate([db_high, db_low, db_high, jnp.zeros((8, BLOCK), bf16)], axis=0)
        grad[pl.ds(k, BLOCK, stride=32), :] = lax.dot_general(
            left, weights, TN, preferred_element_type=f32
        )

    def rows(step, carry):
        x = pair_ref[pl.ds(step * 16, 16)].astype(f32).reshape(512, BLOCK)
        centered = x - jnp.mean(x, axis=-1, keepdims=True)
        reciprocal = lax.rsqrt(jnp.mean(centered * centered, axis=-1, keepdims=True) + EPS)
        normalized = centered * reciprocal
        scaled = grad[pl.ds(pl.multiple_of(step * 512, 512), 512), :]
        second = jnp.mean(scaled * normalized, axis=-1, keepdims=True)
        result = reciprocal * (scaled - normalized * second)
        out_ref[pl.ds(step * 16, 16)] = result.astype(bf16).reshape(16, 32, BLOCK)
        return carry

    lax.fori_loop(0, 8, rows, 0)


def pair_call(pair, gain, weight, pieces):
    return pl.pallas_call(
        pair_kernel,
        out_shape=jax.ShapeDtypeStruct(pair.shape, bf16),
        scratch_shapes=[pltpu.VMEM((4096, BLOCK), f32), pltpu.VMEM((32, 8, BLOCK), f32)],
        compiler_params=pltpu.CompilerParams(vmem_limit_bytes=VMEM_LIMIT),
        cost_estimate=pl.CostEstimate(
            flops=60_000_000, bytes_accessed=2_200_000, transcendentals=4096
        ),
        name="pair_backward",
    )(pair, gain, weight, *pieces)


def along(value, axis, step):
    size = 2 if axis in ("core", "z") else 4
    return lax.ppermute(value, axis, [(p, (p + step) % size) for p in range(size)])


def per_device(
    group, pair, mask, ln_gain, ln_shift, w_query, w_key, w_value, w_gate, gate_bias, w_bias,
    w_out, cotangent,
):
    gain, shift = ln_gain.reshape(1, BLOCK), ln_shift.reshape(1, BLOCK)
    half = 2 * group.shape[0]
    *sent, coef = front_call(
        group, cotangent, pair, gain, shift, w_query, w_key, w_value, w_gate,
        gate_bias.reshape(1, BLOCK), w_out, w_bias,
    )
    pieces = [sent[0]] + [along(sent[d], "y", d) for d in range(1, 4)]
    own = jnp.stack([p[2 * half] for p in pieces])
    gathered = [own] + [along(own, "zh", d) for d in range(1, 4)]
    key_value = jnp.stack([p[:half] for p in pieces])
    gathered, key_value = lax.optimization_barrier((gathered, key_value))
    near = jnp.stack(gathered)
    line, kv_other = lax.optimization_barrier(
        ([near] + [along(near, "x", d) for d in range(1, 4)], along(key_value, "z", 1))
    )
    plane = jnp.stack(line)
    other = along(plane, "core", 1)

    out_own, out_other, out_q, keep, send = attention_call(
        mask.reshape(-1, BLOCK), plane, other, pieces, kv_other
    )

    first = add_core(keep, along(send, "core", 1))
    came = along(out_other, "z", 1)
    second = add_four(first[0], *(along(first[d], "x", -d) for d in range(1, 4)))
    third = [along(second[d], "zh", -d) for d in range(1, 4)]
    packed = pack_call(second[0], *third, out_own, came, out_q)
    back = [packed[0]] + [along(packed[d], "y", -d) for d in range(1, 4)]

    grad_group = group_call(group, gain, w_query, w_key, w_value, w_gate, coef, back)
    grad_pair = pair_call(pair, gain, w_bias, back)
    return (grad_group, grad_pair)


def solution(mesh):
    fine = jax.sharding.Mesh(mesh.devices.reshape(4, 4, 2, 2, 4), ("x", "zh", "core", "z", "y"))
    row, col = ("x", "zh", "core"), ("z", "y")
    placed = (
        P(row, col, None),
        P(col, row, None),
        P(), P(), P(), P(), P(), P(), P(), P(), P(), P(),
        P(row, col, None),
    )
    return jax.shard_map(
        per_device,
        mesh=fine,
        in_specs=placed,
        out_specs=(P(row, col, None), P(col, row, None)),
        check_vma=False,
    )
```

```python
import jax
import jax.numpy as jnp
from jax import lax
from jax.experimental import pallas as pl
from jax.experimental.pallas import tpu as pltpu
from jax.sharding import PartitionSpec as P

HEADS = 4
HEAD_DIM = 32
BLOCK = 128
EPS = 1e-05
SCALE = HEAD_DIM ** (-0.5)
VMEM_LIMIT = 48 * 1024 * 1024

bf16, f32 = jnp.bfloat16, jnp.float32
NT = (((1,), (1,)), ((), ()))
TN = (((0,), (0,)), ((), ()))


def split_high_low(value):
    high = value.astype(bf16)
    return high, (value - high.astype(f32)).astype(bf16)


def fetch(pairs, sems):
    copies = [pltpu.make_async_copy(src, dst, sems.at[n]) for n, (src, dst) in enumerate(pairs)]
    for copy in copies:
        copy.start()
    return copies


def bias_kernel(
    pair_hbm, gain_ref, shift_ref, weight_ref, out_ref, pair_ref, normed, heads, sems
):
    chunks = [pl.ds(16 * n, 16) for n in range(8)]
    copies = fetch([(pair_hbm.at[at], pair_ref.at[at]) for at in chunks], sems)
    gain, shift = gain_ref[...], shift_ref[...]
    weight_t = jnp.concatenate(
        [weight_ref[...].astype(f32), jnp.zeros((16 - HEADS, BLOCK), f32)], axis=0
    ).astype(bf16)

    for n, copy in enumerate(copies):
        copy.wait()
        x = pair_ref[16 * n : 16 * (n + 1)].astype(f32).reshape(512, BLOCK)
        centered = x - jnp.mean(x, axis=-1, keepdims=True)
        reciprocal = lax.rsqrt(jnp.mean(centered * centered, axis=-1, keepdims=True) + EPS)
        low = (centered * reciprocal * gain + shift).astype(bf16).astype(f32)
        normed[512 * n : 512 * (n + 1), :] = low

    for k in range(32):
        block = normed[pl.ds(k, BLOCK, stride=32), :].astype(bf16)
        product = lax.dot_general(weight_t, block, NT, preferred_element_type=f32)
        for h in range(HEADS):
            heads[h, k : k + 1, :] = product[h : h + 1]
    for zh in range(4):
        out_ref[zh] = heads[...].astype(bf16)


def bias_call(pair, gain, shift, weight):
    vmem, hbm = pl.BlockSpec(memory_space=pltpu.VMEM), pl.BlockSpec(memory_space=pltpu.HBM)
    return pl.pallas_call(
        bias_kernel,
        out_shape=jax.ShapeDtypeStruct((4, HEADS, 32, BLOCK), bf16),
        in_specs=[hbm, vmem, vmem, vmem],
        scratch_shapes=[
            pltpu.VMEM(pair.shape, bf16),
            pltpu.VMEM((4096, BLOCK), f32),
            pltpu.VMEM((HEADS, 32, BLOCK), f32),
            pltpu.SemaphoreType.DMA((8,)),
        ],
        compiler_params=pltpu.CompilerParams(vmem_limit_bytes=VMEM_LIMIT),
        cost_estimate=pl.CostEstimate(
            flops=20_000_000, bytes_accessed=1_200_000, transcendentals=4096
        ),
        name="pair_bias",
    )(pair, gain, shift, weight)


def project_kernel(
    group_hbm, cot_hbm, gain_ref, shift_ref, wq_hbm, wk_hbm, wv_hbm, wg_hbm, gb_ref, wo_hbm,
    s0, s1, s2, s3, coef, group_ref, cot_ref, square, parts, sems,
):
    copies = fetch(
        [(wq_hbm, square.at[0]), (wk_hbm, square.at[1]), (wv_hbm, square.at[2]),
         (wg_hbm, square.at[3]), (wo_hbm, square.at[4]), (group_hbm, group_ref),
         (cot_hbm, cot_ref)], sems,
    )
    y = lax.axis_index("y")
    gain, shift = gain_ref[...], shift_ref[...]
    gate_bias = jnp.broadcast_to(gb_ref[...], (BLOCK, BLOCK)).T
    for copy in copies:
        copy.wait()
    turned = [square[n].astype(f32).T.astype(bf16) for n in range(4)]
    rows = group_ref.shape[0]
    for i in range(rows):
        x = group_ref[i].astype(f32)
        centered = x - jnp.mean(x, axis=-1, keepdims=True)
        reciprocal = lax.rsqrt(jnp.mean(centered * centered, axis=-1, keepdims=True) + EPS)
        low = (centered * reciprocal * gain + shift).astype(bf16)
        dots = [lax.dot_general(w, low, NT, preferred_element_type=f32) for w in turned]
        gating = jax.nn.sigmoid(dots[3] + gate_bias)
        gated = lax.dot_general(square[4], cot_ref[i], NT, preferred_element_type=f32)
        upstream = gated * gating
        coef[i] = upstream * (1.0 - gating)
        for n, value in enumerate((dots[1], dots[2], dots[0] * SCALE, upstream)):
            value = value.astype(bf16).reshape(HEADS, HEAD_DIM, BLOCK)
            for h in range(HEADS):
                parts[h, n * rows + i] = value[h]
    for step, out in enumerate((s0, s1, s2, s3)):
        out[...] = parts[lax.rem(y + step, 4)]


def project_call(group, cotangent, gain, shift, wq, wk, wv, wg, gate_bias, wo):
    rows = group.shape[0]
    sent = jax.ShapeDtypeStruct((4 * rows, HEAD_DIM, BLOCK), bf16)
    vmem, hbm = pl.BlockSpec(memory_space=pltpu.VMEM), pl.BlockSpec(memory_space=pltpu.HBM)
    return pl.pallas_call(
        project_kernel,
        out_shape=(sent,) * 4 + (jax.ShapeDtypeStruct((rows, BLOCK, BLOCK), f32),),
        in_specs=[hbm, hbm, vmem, vmem, hbm, hbm, hbm, hbm, vmem, hbm],
        scratch_shapes=[
            pltpu.VMEM(group.shape, bf16),
            pltpu.VMEM(group.shape, bf16),
            pltpu.VMEM((5, BLOCK, BLOCK), bf16),
            pltpu.VMEM((HEADS, 4 * rows, HEAD_DIM, BLOCK), bf16),
            pltpu.SemaphoreType.DMA((7,)),
        ],
        compiler_params=pltpu.CompilerParams(vmem_limit_bytes=VMEM_LIMIT),
        cost_estimate=pl.CostEstimate(
            flops=110_000_000, bytes_accessed=2_000_000, transcendentals=100_000
        ),
        name="project",
    )(group, cotangent, gain, shift, wq, wk, wv, wg, gate_bias, wo)


def attention_kernel(
    mask_ref, bias_own, bias_other, s0, s1, s2, s3, kv_other,
    out_own, out_other, out_q, keep, send,
    bias, grad, key_t, value_t, key_s, value_s, query_t, up_t, key_out, query_out,
):
    x, core, z, y = (lax.axis_index(name) for name in ("x", "core", "z", "y"))
    keys, queries = bias.shape
    rows = key_t.shape[0]

    for blk in range(keys // BLOCK):
        live = jnp.broadcast_to(mask_ref[blk : blk + 1, :].astype(f32), (BLOCK, BLOCK)).T
        bias[blk * BLOCK : (blk + 1) * BLOCK, :] = jnp.concatenate([live] * (queries // BLOCK), 1)
    for source, c in ((bias_own, core), (bias_other, 1 - core)):
        for dx in range(4):
            for zh in range(4):
                r = lax.rem(x - dx + 4, 4) * 8 + zh * 2 + c
                at = pl.ds(pl.multiple_of(r * 32, 32), 32)
                for n in range(4):
                    lanes = slice(n * BLOCK, (n + 1) * BLOCK)
                    bias[at, lanes] = jnp.where(
                        bias[at, lanes] > 0.0, source[dx, zh, n].astype(f32), -jnp.inf
                    )
    grad[...] = jnp.zeros_like(grad)

    for step, own in enumerate((s0, s1, s2, s3)):
        yy = lax.rem(y - step + 4, 4)
        for source, c in ((own, z * 4 + yy), (kv_other.at[step], (1 - z) * 4 + yy)):
            at = pl.ds(pl.multiple_of(c * BLOCK, BLOCK), BLOCK)
            for i in range(rows):
                k, v = source[i], source[rows + i]
                key_t[i, :, at] = k
                value_t[i, :, at] = v
                key_s[i, at, :] = k.astype(f32).T.astype(bf16)
                value_s[i, at, :] = v.astype(f32).T.astype(bf16)
        at = pl.ds(pl.multiple_of(yy * BLOCK, BLOCK), BLOCK)
        for i in range(rows):
            query_t[i, :, at] = own[2 * rows + i]
            up_t[i, :, at] = own[3 * rows + i]

    width = 256

    def row(i, carry):
        grad_key = jnp.zeros((keys, HEAD_DIM), f32)
        grad_value = jnp.zeros((keys, HEAD_DIM), f32)
        for part in range(queries // width):
            lanes = slice(part * width, (part + 1) * width)
            q, g = query_t[i, :, lanes], up_t[i, :, lanes]
            scores = jnp.dot(key_s[i], q, preferred_element_type=f32) + bias[:, lanes]
            raised = jnp.exp(scores)
            weights = raised * (1.0 / jnp.sum(raised, axis=0, keepdims=True))
            low = weights.astype(bf16)
            attended = jnp.dot(value_t[i], low, preferred_element_type=f32)
            delta = jnp.sum(g.astype(f32) * attended, axis=0, keepdims=True)
            grad_weights = jnp.dot(value_s[i], g, preferred_element_type=f32)
            grad_scores = weights * (grad_weights - delta)
            grad[:, lanes] += grad_scores
            scores_low = grad_scores.astype(bf16)
            grad_query = jnp.dot(key_t[i], scores_low, preferred_element_type=f32) * SCALE
            grad_key += lax.dot_general(scores_low, q, NT, preferred_element_type=f32)
            grad_value += lax.dot_general(low, g, NT, preferred_element_type=f32)
            query_out[i, 0, :, lanes] = grad_query.astype(bf16)
            query_out[i, 1, :, lanes] = attended.astype(bf16)
        both = jnp.concatenate([grad_key, grad_value], axis=1).T.astype(bf16)
        key_out[i, 0] = both[:HEAD_DIM]
        key_out[i, 1] = both[HEAD_DIM:]
        return carry

    lax.fori_loop(0, rows, row, 0)

    for step in range(4):
        yy = lax.rem(y - step + 4, 4)
        for out, c in ((out_own, z * 4 + yy), (out_other, (1 - z) * 4 + yy)):
            at = pl.ds(pl.multiple_of(c * BLOCK, BLOCK), BLOCK)
            for i in range(rows):
                out[step, i] = key_out[i, 0, :, at]
                out[step, rows + i] = key_out[i, 1, :, at]
        at = pl.ds(pl.multiple_of(yy * BLOCK, BLOCK), BLOCK)
        for i in range(rows):
            out_q[step, i] = query_out[i, 0, :, at]
            out_q[step, rows + i] = query_out[i, 1, :, at]
    for out, c in ((keep, core), (send, 1 - core)):
        for dx in range(4):
            for zh in range(4):
                r = lax.rem(x - dx + 4, 4) * 8 + zh * 2 + c
                at = pl.ds(pl.multiple_of(r * 32, 32), 32)
                for n in range(4):
                    piece = grad[at, n * BLOCK : (n + 1) * BLOCK]
                    out[dx, zh, n] = piece.astype(out.dtype)


def attention_call(mask, bias_own, bias_other, pieces, kv_other):
    rows = kv_other.shape[1] // 2
    keys = mask.shape[0] * mask.shape[1]
    queries = keys // 2
    part = jax.ShapeDtypeStruct(kv_other.shape, bf16)
    return pl.pallas_call(
        attention_kernel,
        out_shape=(
            part, part, part,
            jax.ShapeDtypeStruct(bias_own.shape, f32),
            jax.ShapeDtypeStruct(bias_own.shape, bf16),
        ),
        scratch_shapes=[
            pltpu.VMEM((keys, queries), f32),
            pltpu.VMEM((keys, queries), f32),
            pltpu.VMEM((rows, HEAD_DIM, keys), bf16),
            pltpu.VMEM((rows, HEAD_DIM, keys), bf16),
            pltpu.VMEM((rows, keys, HEAD_DIM), bf16),
            pltpu.VMEM((rows, keys, HEAD_DIM), bf16),
            pltpu.VMEM((rows, HEAD_DIM, queries), bf16),
            pltpu.VMEM((rows, HEAD_DIM, queries), bf16),
            pltpu.VMEM((rows, 2, HEAD_DIM, keys), bf16),
            pltpu.VMEM((rows, 2, HEAD_DIM, queries), bf16),
        ],
        compiler_params=pltpu.CompilerParams(vmem_limit_bytes=VMEM_LIMIT),
        cost_estimate=pl.CostEstimate(
            flops=8_000_000_000, bytes_accessed=6_000_000, transcendentals=2_700_000
        ),
        name="attention",
    )(mask, bias_own, bias_other, *pieces, kv_other)


def add_core_kernel(keep, came, k0, s1, s2, s3):
    for n, out in enumerate((k0, s1, s2, s3)):
        out[...] = (keep[n] + came[n].astype(f32)).astype(out.dtype)


def add_core(keep, came):
    shape = keep.shape[1:]
    return pl.pallas_call(
        add_core_kernel,
        out_shape=(jax.ShapeDtypeStruct(shape, f32),) + (jax.ShapeDtypeStruct(shape, bf16),) * 3,
        compiler_params=pltpu.CompilerParams(vmem_limit_bytes=VMEM_LIMIT),
        name="add_core",
    )(keep, came)


def add_four_kernel(keep, c1, c2, c3, out):
    total = (keep[...] + c1[...].astype(f32)) + (c2[...].astype(f32) + c3[...].astype(f32))
    out[...] = total.astype(bf16)


def add_four(keep, c1, c2, c3):
    return pl.pallas_call(
        add_four_kernel,
        out_shape=jax.ShapeDtypeStruct(keep.shape, bf16),
        compiler_params=pltpu.CompilerParams(vmem_limit_bytes=VMEM_LIMIT),
        name="add_four",
    )(keep, c1, c2, c3)


def pack_kernel(own, came, query, t0, t1, t2, t3):
    half = own.shape[1]
    for n, out in enumerate((t0, t1, t2, t3)):
        out[:half] = (own[n].astype(f32) + came[n].astype(f32)).astype(bf16)
        out[half:] = query[n]


def pack_call(own, came, query):
    half, *tile = own.shape[1:]
    return pl.pallas_call(
        pack_kernel,
        out_shape=(jax.ShapeDtypeStruct((2 * half, *tile), bf16),) * 4,
        compiler_params=pltpu.CompilerParams(vmem_limit_bytes=VMEM_LIMIT),
        name="pack",
    )(own, came, query)


def group_kernel(
    group_ref, gain_ref, wq_ref, wk_ref, wv_ref, wg_ref, coef,
    t0, t1, t2, t3, out_ref,
):
    y = lax.axis_index("y")
    gain = gain_ref[...]
    turn = lax.rem(4 - y, 4) * HEAD_DIM
    wq, wk, wv, wg = (
        pltpu.roll(w[...].astype(f32), turn, 1).astype(bf16)
        for w in (wq_ref, wk_ref, wv_ref, wg_ref)
    )
    weights = jnp.concatenate([wk, wv, wq, wg, wg], axis=1)
    rows = group_ref.shape[0]
    for i in range(rows):
        parts = [[] for _ in range(5)]
        for step, t in enumerate((t0, t1, t2, t3)):
            h = lax.rem(y + step, 4)
            at = pl.multiple_of(h * HEAD_DIM, HEAD_DIM)
            gate = coef[i, pl.ds(at, HEAD_DIM), :] * t[3 * rows + i].astype(f32)
            high, low = split_high_low(gate)
            pieces = (t[i], t[rows + i], t[2 * rows + i], high, low)
            for part, piece in zip(parts, pieces):
                part.append(piece)
        stacked = jnp.concatenate(sum(parts, []), axis=0)
        upstream = jnp.dot(weights, stacked, preferred_element_type=f32).T
        x = group_ref[i].astype(f32)
        centered = x - jnp.mean(x, axis=-1, keepdims=True)
        reciprocal = lax.rsqrt(jnp.mean(centered * centered, axis=-1, keepdims=True) + EPS)
        normalized = centered * reciprocal
        scaled = upstream * gain
        first = jnp.mean(scaled, axis=-1, keepdims=True)
        second = jnp.mean(scaled * normalized, axis=-1, keepdims=True)
        out_ref[i] = (reciprocal * (scaled - first - normalized * second)).astype(bf16)


def group_call(group, gain, wq, wk, wv, wg, coef, pieces):
    return pl.pallas_call(
        group_kernel,
        out_shape=jax.ShapeDtypeStruct(group.shape, bf16),
        compiler_params=pltpu.CompilerParams(vmem_limit_bytes=VMEM_LIMIT),
        cost_estimate=pl.CostEstimate(
            flops=160_000_000, bytes_accessed=2_000_000, transcendentals=1000
        ),
        name="group_backward",
    )(group, gain, wq, wk, wv, wg, coef, *pieces)


def pair_kernel(pair_ref, gain_ref, weight_ref, came, out_ref, grad, db):
    weight = jnp.concatenate(
        [weight_ref[...].astype(f32), jnp.zeros((8 - HEADS, BLOCK), f32)], axis=0
    ) * gain_ref[...]
    weight = weight - jnp.mean(weight, axis=-1, keepdims=True)
    high, low = split_high_low(weight)
    weights = jnp.concatenate([high, high, low, jnp.zeros((8, BLOCK), bf16)], axis=0)
    db[...] = jnp.zeros_like(db)
    for h in range(HEADS):
        wide = [came[zh, h].astype(f32) for zh in range(4)]
        value = (wide[0] + wide[1]) + (wide[2] + wide[3])
        for k in range(32):
            db[k, h : h + 1, :] = value[k : k + 1]

    for k in range(32):
        db_high, db_low = split_high_low(db[k])
        left = jnp.concatenate([db_high, db_low, db_high, jnp.zeros((8, BLOCK), bf16)], axis=0)
        grad[pl.ds(k, BLOCK, stride=32), :] = lax.dot_general(
            left, weights, TN, preferred_element_type=f32
        )

    def rows(step, carry):
        x = pair_ref[pl.ds(step * 16, 16)].astype(f32).reshape(512, BLOCK)
        centered = x - jnp.mean(x, axis=-1, keepdims=True)
        reciprocal = lax.rsqrt(jnp.mean(centered * centered, axis=-1, keepdims=True) + EPS)
        normalized = centered * reciprocal
        scaled = grad[pl.ds(pl.multiple_of(step * 512, 512), 512), :]
        second = jnp.mean(scaled * normalized, axis=-1, keepdims=True)
        result = reciprocal * (scaled - normalized * second)
        out_ref[pl.ds(step * 16, 16)] = result.astype(bf16).reshape(16, 32, BLOCK)
        return carry

    lax.fori_loop(0, 8, rows, 0)


def pair_call(pair, gain, weight, came):
    return pl.pallas_call(
        pair_kernel,
        out_shape=jax.ShapeDtypeStruct(pair.shape, bf16),
        scratch_shapes=[pltpu.VMEM((4096, BLOCK), f32), pltpu.VMEM((32, 8, BLOCK), f32)],
        compiler_params=pltpu.CompilerParams(vmem_limit_bytes=VMEM_LIMIT),
        cost_estimate=pl.CostEstimate(
            flops=60_000_000, bytes_accessed=2_200_000, transcendentals=4096
        ),
        name="pair_backward",
    )(pair, gain, weight, came)


def along(value, axis, step):
    size = 2 if axis in ("core", "z") else 4
    return lax.ppermute(value, axis, [(p, (p + step) % size) for p in range(size)])


def exchange(value):
    flat = value.reshape(16, *value.shape[2:])
    flat = lax.all_to_all(flat, ("zh", "y"), split_axis=0, concat_axis=0, tiled=True)
    return flat.reshape(value.shape)


def per_device(
    group, pair, mask, ln_gain, ln_shift, w_query, w_key, w_value, w_gate, gate_bias, w_bias,
    w_out, cotangent,
):
    gain, shift = ln_gain.reshape(1, BLOCK), ln_shift.reshape(1, BLOCK)
    half = 2 * group.shape[0]
    bias = bias_call(pair, gain, shift, w_bias.T)
    bias, group, cotangent = lax.optimization_barrier((bias, group, cotangent))
    near = exchange(bias)

    *sent, coef = project_call(
        group, cotangent, gain, shift, w_query, w_key, w_value, w_gate,
        gate_bias.reshape(1, BLOCK), w_out,
    )
    pieces = [sent[0]] + [along(sent[d], "y", d) for d in range(1, 4)]
    key_value = jnp.stack([p[:half] for p in pieces])
    line, kv_other = lax.optimization_barrier(
        ([near] + [along(near, "x", d) for d in range(1, 4)], along(key_value, "z", 1))
    )
    plane = jnp.stack(line)
    other = along(plane, "core", 1)

    out_own, out_other, out_q, keep, send = attention_call(
        mask.reshape(-1, BLOCK), plane, other, pieces, kv_other
    )

    first = add_core(keep, along(send, "core", 1))
    came = along(out_other, "z", 1)
    second = add_four(first[0], *(along(first[d], "x", -d) for d in range(1, 4)))
    grad_bias = exchange(second)
    packed = pack_call(out_own, came, out_q)
    back = [packed[0]] + [along(packed[d], "y", -d) for d in range(1, 4)]

    grad_group = group_call(group, gain, w_query, w_key, w_value, w_gate, coef, back)
    grad_pair = pair_call(pair, gain, w_bias.T, grad_bias)
    return (grad_group, grad_pair)


def solution(mesh):
    fine = jax.sharding.Mesh(mesh.devices.reshape(4, 4, 2, 2, 4), ("x", "zh", "core", "z", "y"))
    row, col = ("x", "zh", "core"), ("z", "y")
    placed = (
        P(row, col, None),
        P(col, row, None),
        P(), P(), P(), P(), P(), P(), P(), P(), P(), P(),
        P(row, col, None),
    )
    return jax.shard_map(
        per_device,
        mesh=fine,
        in_specs=placed,
        out_specs=(P(row, col, None), P(col, row, None)),
        check_vma=False,
    )
```

```python
import jax
import jax.numpy as jnp
from jax import lax
from jax.experimental import pallas as pl
from jax.experimental.pallas import tpu as pltpu
from jax.sharding import PartitionSpec as P

HEADS = 4
HEAD_DIM = 32
BLOCK = 128
EPS = 1e-05
SCALE = HEAD_DIM ** (-0.5)
VMEM_LIMIT = 48 * 1024 * 1024

bf16, f32 = jnp.bfloat16, jnp.float32
NT = (((1,), (1,)), ((), ()))
TN = (((0,), (0,)), ((), ()))


def split_high_low(value):
    high = value.astype(bf16)
    return high, (value - high.astype(f32)).astype(bf16)


def bias_kernel(pair_ref, gain_ref, shift_ref, weight_ref, out_ref, normed, heads):
    gain, shift = gain_ref[...], shift_ref[...]
    weight_t = jnp.concatenate(
        [weight_ref[...].astype(f32), jnp.zeros((16 - HEADS, BLOCK), f32)], axis=0
    ).astype(bf16)

    def rows(step, carry):
        x = pair_ref[pl.ds(step * 16, 16)].astype(f32).reshape(512, BLOCK)
        centered = x - jnp.mean(x, axis=-1, keepdims=True)
        reciprocal = lax.rsqrt(jnp.mean(centered * centered, axis=-1, keepdims=True) + EPS)
        low = (centered * reciprocal * gain + shift).astype(bf16).astype(f32)
        normed[pl.ds(pl.multiple_of(step * 512, 512), 512), :] = low
        return carry

    lax.fori_loop(0, 8, rows, 0)

    for k in range(32):
        block = normed[pl.ds(k, BLOCK, stride=32), :].astype(bf16)
        product = lax.dot_general(weight_t, block, NT, preferred_element_type=f32)
        for h in range(HEADS):
            heads[h, k : k + 1, :] = product[h : h + 1]
    for zh in range(4):
        out_ref[zh] = heads[...].astype(bf16)


def bias_call(pair, gain, shift, weight):
    return pl.pallas_call(
        bias_kernel,
        out_shape=jax.ShapeDtypeStruct((4, HEADS, 32, BLOCK), bf16),
        scratch_shapes=[pltpu.VMEM((4096, BLOCK), f32), pltpu.VMEM((HEADS, 32, BLOCK), f32)],
        compiler_params=pltpu.CompilerParams(vmem_limit_bytes=VMEM_LIMIT),
        cost_estimate=pl.CostEstimate(
            flops=20_000_000, bytes_accessed=1_200_000, transcendentals=4096
        ),
        name="pair_bias",
    )(pair, gain, shift, weight)


def project_kernel(
    group_ref, cot_ref, gain_ref, shift_ref, wq_ref, wk_ref, wv_ref, wg_ref, gb_ref, wo_ref,
    s0, s1, s2, s3, coef, parts,
):
    y = lax.axis_index("y")
    gain, shift = gain_ref[...], shift_ref[...]
    gate_bias = jnp.broadcast_to(gb_ref[...], (BLOCK, BLOCK)).T
    turned = [w[...].astype(f32).T.astype(bf16) for w in (wq_ref, wk_ref, wv_ref, wg_ref)]
    rows = group_ref.shape[0]
    for i in range(rows):
        x = group_ref[i].astype(f32)
        centered = x - jnp.mean(x, axis=-1, keepdims=True)
        reciprocal = lax.rsqrt(jnp.mean(centered * centered, axis=-1, keepdims=True) + EPS)
        low = (centered * reciprocal * gain + shift).astype(bf16)
        dots = [lax.dot_general(w, low, NT, preferred_element_type=f32) for w in turned]
        gating = jax.nn.sigmoid(dots[3] + gate_bias)
        gated = lax.dot_general(wo_ref[...], cot_ref[i], NT, preferred_element_type=f32)
        upstream = gated * gating
        coef[i] = upstream * (1.0 - gating)
        for n, value in enumerate((dots[1], dots[2], dots[0] * SCALE, upstream)):
            value = value.astype(bf16).reshape(HEADS, HEAD_DIM, BLOCK)
            for h in range(HEADS):
                parts[h, n * rows + i] = value[h]
    for step, out in enumerate((s0, s1, s2, s3)):
        out[...] = parts[lax.rem(y + step, 4)]


def project_call(group, cotangent, gain, shift, wq, wk, wv, wg, gate_bias, wo):
    rows = group.shape[0]
    sent = jax.ShapeDtypeStruct((4 * rows, HEAD_DIM, BLOCK), bf16)
    return pl.pallas_call(
        project_kernel,
        out_shape=(sent,) * 4 + (jax.ShapeDtypeStruct((rows, BLOCK, BLOCK), f32),),
        scratch_shapes=[pltpu.VMEM((HEADS, 4 * rows, HEAD_DIM, BLOCK), bf16)],
        compiler_params=pltpu.CompilerParams(vmem_limit_bytes=VMEM_LIMIT),
        cost_estimate=pl.CostEstimate(
            flops=110_000_000, bytes_accessed=2_000_000, transcendentals=100_000
        ),
        name="project",
    )(group, cotangent, gain, shift, wq, wk, wv, wg, gate_bias, wo)


def attention_kernel(
    mask_ref, bias_own, bias_other, s0, s1, s2, s3, kv_other,
    out_own, out_other, out_q, keep, send,
    bias, grad, key_t, value_t, key_s, value_s, query_t, up_t, key_out, query_out,
):
    x, core, z, y = (lax.axis_index(name) for name in ("x", "core", "z", "y"))
    keys, queries = bias.shape
    rows = key_t.shape[0]

    for blk in range(keys // BLOCK):
        live = jnp.broadcast_to(mask_ref[blk : blk + 1, :].astype(f32), (BLOCK, BLOCK)).T
        bias[blk * BLOCK : (blk + 1) * BLOCK, :] = jnp.concatenate([live] * (queries // BLOCK), 1)
    for source, c in ((bias_own, core), (bias_other, 1 - core)):
        for dx in range(4):
            for zh in range(4):
                r = lax.rem(x - dx + 4, 4) * 8 + zh * 2 + c
                at = pl.ds(pl.multiple_of(r * 32, 32), 32)
                for n in range(4):
                    lanes = slice(n * BLOCK, (n + 1) * BLOCK)
                    bias[at, lanes] = jnp.where(
                        bias[at, lanes] > 0.0, source[dx, zh, n].astype(f32), -jnp.inf
                    )
    grad[...] = jnp.zeros_like(grad)

    for step, own in enumerate((s0, s1, s2, s3)):
        yy = lax.rem(y - step + 4, 4)
        for source, c in ((own, z * 4 + yy), (kv_other.at[step], (1 - z) * 4 + yy)):
            at = pl.ds(pl.multiple_of(c * BLOCK, BLOCK), BLOCK)
            for i in range(rows):
                k, v = source[i], source[rows + i]
                key_t[i, :, at] = k
                value_t[i, :, at] = v
                key_s[i, at, :] = k.astype(f32).T.astype(bf16)
                value_s[i, at, :] = v.astype(f32).T.astype(bf16)
        at = pl.ds(pl.multiple_of(yy * BLOCK, BLOCK), BLOCK)
        for i in range(rows):
            query_t[i, :, at] = own[2 * rows + i]
            up_t[i, :, at] = own[3 * rows + i]

    width = 256

    def row(i, carry):
        grad_key = jnp.zeros((keys, HEAD_DIM), f32)
        grad_value = jnp.zeros((keys, HEAD_DIM), f32)
        for part in range(queries // width):
            lanes = slice(part * width, (part + 1) * width)
            q, g = query_t[i, :, lanes], up_t[i, :, lanes]
            scores = jnp.dot(key_s[i], q, preferred_element_type=f32) + bias[:, lanes]
            raised = jnp.exp(scores)
            weights = raised * (1.0 / jnp.sum(raised, axis=0, keepdims=True))
            low = weights.astype(bf16)
            attended = jnp.dot(value_t[i], low, preferred_element_type=f32)
            delta = jnp.sum(g.astype(f32) * attended, axis=0, keepdims=True)
            grad_weights = jnp.dot(value_s[i], g, preferred_element_type=f32)
            grad_scores = weights * (grad_weights - delta)
            grad[:, lanes] += grad_scores
            scores_low = grad_scores.astype(bf16)
            grad_query = jnp.dot(key_t[i], scores_low, preferred_element_type=f32) * SCALE
            grad_key += lax.dot_general(scores_low, q, NT, preferred_element_type=f32)
            grad_value += lax.dot_general(low, g, NT, preferred_element_type=f32)
            query_out[i, 0, :, lanes] = grad_query.astype(bf16)
            query_out[i, 1, :, lanes] = attended.astype(bf16)
        both = jnp.concatenate([grad_key, grad_value], axis=1).T.astype(bf16)
        key_out[i, 0] = both[:HEAD_DIM]
        key_out[i, 1] = both[HEAD_DIM:]
        return carry

    lax.fori_loop(0, rows, row, 0)

    for step in range(4):
        yy = lax.rem(y - step + 4, 4)
        for out, c in ((out_own, z * 4 + yy), (out_other, (1 - z) * 4 + yy)):
            at = pl.ds(pl.multiple_of(c * BLOCK, BLOCK), BLOCK)
            for i in range(rows):
                out[step, i] = key_out[i, 0, :, at]
                out[step, rows + i] = key_out[i, 1, :, at]
        at = pl.ds(pl.multiple_of(yy * BLOCK, BLOCK), BLOCK)
        for i in range(rows):
            out_q[step, i] = query_out[i, 0, :, at]
            out_q[step, rows + i] = query_out[i, 1, :, at]
    for out, c in ((keep, core), (send, 1 - core)):
        for dx in range(4):
            for zh in range(4):
                r = lax.rem(x - dx + 4, 4) * 8 + zh * 2 + c
                at = pl.ds(pl.multiple_of(r * 32, 32), 32)
                for n in range(4):
                    piece = grad[at, n * BLOCK : (n + 1) * BLOCK]
                    out[dx, zh, n] = piece.astype(out.dtype)


def attention_call(mask, bias_own, bias_other, pieces, kv_other):
    rows = kv_other.shape[1] // 2
    keys = mask.shape[0] * mask.shape[1]
    queries = keys // 2
    part = jax.ShapeDtypeStruct(kv_other.shape, bf16)
    return pl.pallas_call(
        attention_kernel,
        out_shape=(
            part, part, part,
            jax.ShapeDtypeStruct(bias_own.shape, f32),
            jax.ShapeDtypeStruct(bias_own.shape, bf16),
        ),
        scratch_shapes=[
            pltpu.VMEM((keys, queries), f32),
            pltpu.VMEM((keys, queries), f32),
            pltpu.VMEM((rows, HEAD_DIM, keys), bf16),
            pltpu.VMEM((rows, HEAD_DIM, keys), bf16),
            pltpu.VMEM((rows, keys, HEAD_DIM), bf16),
            pltpu.VMEM((rows, keys, HEAD_DIM), bf16),
            pltpu.VMEM((rows, HEAD_DIM, queries), bf16),
            pltpu.VMEM((rows, HEAD_DIM, queries), bf16),
            pltpu.VMEM((rows, 2, HEAD_DIM, keys), bf16),
            pltpu.VMEM((rows, 2, HEAD_DIM, queries), bf16),
        ],
        compiler_params=pltpu.CompilerParams(vmem_limit_bytes=VMEM_LIMIT),
        cost_estimate=pl.CostEstimate(
            flops=8_000_000_000, bytes_accessed=6_000_000, transcendentals=2_700_000
        ),
        name="attention",
    )(mask, bias_own, bias_other, *pieces, kv_other)


def add_core_kernel(keep, came, k0, s1, s2, s3):
    for n, out in enumerate((k0, s1, s2, s3)):
        out[...] = (keep[n] + came[n].astype(f32)).astype(out.dtype)


def add_core(keep, came):
    shape = keep.shape[1:]
    return pl.pallas_call(
        add_core_kernel,
        out_shape=(jax.ShapeDtypeStruct(shape, f32),) + (jax.ShapeDtypeStruct(shape, bf16),) * 3,
        compiler_params=pltpu.CompilerParams(vmem_limit_bytes=VMEM_LIMIT),
        name="add_core",
    )(keep, came)


def add_four_kernel(keep, c1, c2, c3, out):
    total = (keep[...] + c1[...].astype(f32)) + (c2[...].astype(f32) + c3[...].astype(f32))
    out[...] = total.astype(bf16)


def add_four(keep, c1, c2, c3):
    return pl.pallas_call(
        add_four_kernel,
        out_shape=jax.ShapeDtypeStruct(keep.shape, bf16),
        compiler_params=pltpu.CompilerParams(vmem_limit_bytes=VMEM_LIMIT),
        name="add_four",
    )(keep, c1, c2, c3)


def pack_kernel(own, came, query, t0, t1, t2, t3):
    half = own.shape[1]
    for n, out in enumerate((t0, t1, t2, t3)):
        out[:half] = (own[n].astype(f32) + came[n].astype(f32)).astype(bf16)
        out[half:] = query[n]


def pack_call(own, came, query):
    half, *tile = own.shape[1:]
    return pl.pallas_call(
        pack_kernel,
        out_shape=(jax.ShapeDtypeStruct((2 * half, *tile), bf16),) * 4,
        compiler_params=pltpu.CompilerParams(vmem_limit_bytes=VMEM_LIMIT),
        name="pack",
    )(own, came, query)


def group_kernel(
    group_ref, gain_ref, wq_ref, wk_ref, wv_ref, wg_ref, coef,
    t0, t1, t2, t3, out_ref,
):
    y = lax.axis_index("y")
    gain = gain_ref[...]
    turn = lax.rem(4 - y, 4) * HEAD_DIM
    wq, wk, wv, wg = (
        pltpu.roll(w[...].astype(f32), turn, 1).astype(bf16)
        for w in (wq_ref, wk_ref, wv_ref, wg_ref)
    )
    weights = jnp.concatenate([wk, wv, wq, wg, wg], axis=1)
    rows = group_ref.shape[0]
    for i in range(rows):
        parts = [[] for _ in range(5)]
        for step, t in enumerate((t0, t1, t2, t3)):
            h = lax.rem(y + step, 4)
            at = pl.multiple_of(h * HEAD_DIM, HEAD_DIM)
            gate = coef[i, pl.ds(at, HEAD_DIM), :] * t[3 * rows + i].astype(f32)
            high, low = split_high_low(gate)
            pieces = (t[i], t[rows + i], t[2 * rows + i], high, low)
            for part, piece in zip(parts, pieces):
                part.append(piece)
        stacked = jnp.concatenate(sum(parts, []), axis=0)
        upstream = jnp.dot(weights, stacked, preferred_element_type=f32).T
        x = group_ref[i].astype(f32)
        centered = x - jnp.mean(x, axis=-1, keepdims=True)
        reciprocal = lax.rsqrt(jnp.mean(centered * centered, axis=-1, keepdims=True) + EPS)
        normalized = centered * reciprocal
        scaled = upstream * gain
        first = jnp.mean(scaled, axis=-1, keepdims=True)
        second = jnp.mean(scaled * normalized, axis=-1, keepdims=True)
        out_ref[i] = (reciprocal * (scaled - first - normalized * second)).astype(bf16)


def group_call(group, gain, wq, wk, wv, wg, coef, pieces):
    return pl.pallas_call(
        group_kernel,
        out_shape=jax.ShapeDtypeStruct(group.shape, bf16),
        compiler_params=pltpu.CompilerParams(vmem_limit_bytes=VMEM_LIMIT),
        cost_estimate=pl.CostEstimate(
            flops=160_000_000, bytes_accessed=2_000_000, transcendentals=1000
        ),
        name="group_backward",
    )(group, gain, wq, wk, wv, wg, coef, *pieces)


def pair_kernel(pair_ref, gain_ref, weight_ref, came, out_ref, grad, db):
    weight = jnp.concatenate(
        [weight_ref[...].astype(f32), jnp.zeros((8 - HEADS, BLOCK), f32)], axis=0
    ) * gain_ref[...]
    weight = weight - jnp.mean(weight, axis=-1, keepdims=True)
    high, low = split_high_low(weight)
    weights = jnp.concatenate([high, high, low, jnp.zeros((8, BLOCK), bf16)], axis=0)
    db[...] = jnp.zeros_like(db)
    for h in range(HEADS):
        wide = [came[zh, h].astype(f32) for zh in range(4)]
        value = (wide[0] + wide[1]) + (wide[2] + wide[3])
        for k in range(32):
            db[k, h : h + 1, :] = value[k : k + 1]

    for k in range(32):
        db_high, db_low = split_high_low(db[k])
        left = jnp.concatenate([db_high, db_low, db_high, jnp.zeros((8, BLOCK), bf16)], axis=0)
        grad[pl.ds(k, BLOCK, stride=32), :] = lax.dot_general(
            left, weights, TN, preferred_element_type=f32
        )

    def rows(step, carry):
        x = pair_ref[pl.ds(step * 16, 16)].astype(f32).reshape(512, BLOCK)
        centered = x - jnp.mean(x, axis=-1, keepdims=True)
        reciprocal = lax.rsqrt(jnp.mean(centered * centered, axis=-1, keepdims=True) + EPS)
        normalized = centered * reciprocal
        scaled = grad[pl.ds(pl.multiple_of(step * 512, 512), 512), :]
        second = jnp.mean(scaled * normalized, axis=-1, keepdims=True)
        result = reciprocal * (scaled - normalized * second)
        out_ref[pl.ds(step * 16, 16)] = result.astype(bf16).reshape(16, 32, BLOCK)
        return carry

    lax.fori_loop(0, 8, rows, 0)


def pair_call(pair, gain, weight, came):
    return pl.pallas_call(
        pair_kernel,
        out_shape=jax.ShapeDtypeStruct(pair.shape, bf16),
        scratch_shapes=[pltpu.VMEM((4096, BLOCK), f32), pltpu.VMEM((32, 8, BLOCK), f32)],
        compiler_params=pltpu.CompilerParams(vmem_limit_bytes=VMEM_LIMIT),
        cost_estimate=pl.CostEstimate(
            flops=60_000_000, bytes_accessed=2_200_000, transcendentals=4096
        ),
        name="pair_backward",
    )(pair, gain, weight, came)


def along(value, axis, step):
    size = 2 if axis in ("core", "z") else 4
    return lax.ppermute(value, axis, [(p, (p + step) % size) for p in range(size)])


def exchange(value):
    flat = value.reshape(16, *value.shape[2:])
    flat = lax.all_to_all(flat, ("zh", "y"), split_axis=0, concat_axis=0, tiled=True)
    return flat.reshape(value.shape)


def per_device(
    group, pair, mask, ln_gain, ln_shift, w_query, w_key, w_value, w_gate, gate_bias, w_bias,
    w_out, cotangent,
):
    gain, shift = ln_gain.reshape(1, BLOCK), ln_shift.reshape(1, BLOCK)
    half = 2 * group.shape[0]
    bias = bias_call(pair, gain, shift, w_bias.T)
    bias, group, cotangent = lax.optimization_barrier((bias, group, cotangent))
    *sent, coef = project_call(
        group, cotangent, gain, shift, w_query, w_key, w_value, w_gate,
        gate_bias.reshape(1, BLOCK), w_out,
    )
    pieces = [sent[0]] + [along(sent[d], "y", d) for d in range(1, 4)]
    bias, pieces[1] = lax.optimization_barrier((bias, pieces[1]))
    near = exchange(bias)
    key_value = jnp.stack([p[:half] for p in pieces])
    line, kv_other = lax.optimization_barrier(
        ([near] + [along(near, "x", d) for d in range(1, 4)], along(key_value, "z", 1))
    )
    plane = jnp.stack(line)
    other = along(plane, "core", 1)

    out_own, out_other, out_q, keep, send = attention_call(
        mask.reshape(-1, BLOCK), plane, other, pieces, kv_other
    )

    first = add_core(keep, along(send, "core", 1))
    came = along(out_other, "z", 1)
    first, out_own, out_q = lax.optimization_barrier((first, out_own, out_q))
    packed = pack_call(out_own, came, out_q)
    back = [packed[0]] + [along(packed[d], "y", -d) for d in range(1, 4)]
    sums = [along(first[d], "x", -d) for d in range(1, 4)]
    back, sums = lax.optimization_barrier((back, sums))
    grad_bias = exchange(add_four(first[0], *sums))
    grad_group = group_call(group, gain, w_query, w_key, w_value, w_gate, coef, back)
    grad_pair = pair_call(pair, gain, w_bias.T, grad_bias)
    return (grad_group, grad_pair)


def solution(mesh):
    fine = jax.sharding.Mesh(mesh.devices.reshape(4, 4, 2, 2, 4), ("x", "zh", "core", "z", "y"))
    row, col = ("x", "zh", "core"), ("z", "y")
    placed = (
        P(row, col, None),
        P(col, row, None),
        P(), P(), P(), P(), P(), P(), P(), P(), P(), P(),
        P(row, col, None),
    )
    return jax.shard_map(
        per_device,
        mesh=fine,
        in_specs=placed,
        out_specs=(P(row, col, None), P(col, row, None)),
        check_vma=False,
    )
```

```python
import jax
import jax.numpy as jnp
from jax import lax
from jax.experimental import pallas as pl
from jax.experimental.pallas import tpu as pltpu
from jax.sharding import PartitionSpec as P

HEADS = 4
HEAD_DIM = 32
BLOCK = 128
EPS = 1e-05
SCALE = HEAD_DIM ** (-0.5)
VMEM_LIMIT = 48 * 1024 * 1024

bf16, f32 = jnp.bfloat16, jnp.float32
NT = (((1,), (1,)), ((), ()))
TN = (((0,), (0,)), ((), ()))


def place():
    return tuple(lax.axis_index(name) for name in ("x", "zh", "core", "z", "y"))


def split_high_low(value):
    high = value.astype(bf16)
    return high, (value - high.astype(f32)).astype(bf16)


def bias_kernel(pair_ref, gain_ref, shift_ref, weight_ref, out_ref, normed, heads):
    gain, shift = gain_ref[...], shift_ref[...]
    weight_t = jnp.concatenate(
        [weight_ref[...].astype(f32), jnp.zeros((16 - HEADS, BLOCK), f32)], axis=0
    ).astype(bf16)

    def rows(step, carry):
        x = pair_ref[pl.ds(step * 16, 16)].astype(f32).reshape(512, BLOCK)
        centered = x - jnp.mean(x, axis=-1, keepdims=True)
        reciprocal = lax.rsqrt(jnp.mean(centered * centered, axis=-1, keepdims=True) + EPS)
        low = (centered * reciprocal * gain + shift).astype(bf16).astype(f32)
        normed[pl.ds(pl.multiple_of(step * 512, 512), 512), :] = low
        return carry

    lax.fori_loop(0, 8, rows, 0)

    for k in range(32):
        block = normed[pl.ds(k, BLOCK, stride=32), :].astype(bf16)
        product = lax.dot_general(weight_t, block, NT, preferred_element_type=f32)
        for h in range(HEADS):
            heads[h, k : k + 1, :] = product[h : h + 1]
    y = lax.axis_index("y")
    for step in range(HEADS):
        out_ref[step] = heads[lax.rem(y + step, 4)].astype(bf16)


def bias_call(pair, gain, shift, weight):
    return pl.pallas_call(
        bias_kernel,
        out_shape=jax.ShapeDtypeStruct((HEADS, 32, BLOCK), bf16),
        scratch_shapes=[pltpu.VMEM((4096, BLOCK), f32), pltpu.VMEM((HEADS, 32, BLOCK), f32)],
        compiler_params=pltpu.CompilerParams(vmem_limit_bytes=VMEM_LIMIT),
        cost_estimate=pl.CostEstimate(
            flops=20_000_000, bytes_accessed=1_200_000, transcendentals=4096
        ),
        name="pair_bias",
    )(pair, gain, shift, weight)


def turn_kernel(g0, g1, g2, g3, s0, s1, s2, s3):
    for n, source in enumerate((g0, g1, g2, g3)):
        for step, out in enumerate((s0, s1, s2, s3)):
            out[n] = source[step]


def turn_call(gathered):
    return pl.pallas_call(
        turn_kernel,
        out_shape=(jax.ShapeDtypeStruct(gathered[0].shape, bf16),) * 4,
        compiler_params=pltpu.CompilerParams(vmem_limit_bytes=VMEM_LIMIT),
        name="turn",
    )(*gathered)


def project_kernel(
    group_ref, cot_ref, gain_ref, shift_ref, wq_ref, wk_ref, wv_ref, wg_ref, gb_ref, wo_ref,
    s0, s1, s2, s3, coef, parts,
):
    y = lax.axis_index("y")
    gain, shift = gain_ref[...], shift_ref[...]
    gate_bias = jnp.broadcast_to(gb_ref[...], (BLOCK, BLOCK)).T
    turned = [w[...].astype(f32).T.astype(bf16) for w in (wq_ref, wk_ref, wv_ref, wg_ref)]
    rows = group_ref.shape[0]
    for i in range(rows):
        x = group_ref[i].astype(f32)
        centered = x - jnp.mean(x, axis=-1, keepdims=True)
        reciprocal = lax.rsqrt(jnp.mean(centered * centered, axis=-1, keepdims=True) + EPS)
        low = (centered * reciprocal * gain + shift).astype(bf16)
        dots = [lax.dot_general(w, low, NT, preferred_element_type=f32) for w in turned]
        gating = jax.nn.sigmoid(dots[3] + gate_bias)
        gated = lax.dot_general(wo_ref[...], cot_ref[i], NT, preferred_element_type=f32)
        upstream = gated * gating
        coef[i] = upstream * (1.0 - gating)
        for n, value in enumerate((dots[1], dots[2], dots[0] * SCALE, upstream)):
            value = value.astype(bf16).reshape(HEADS, HEAD_DIM, BLOCK)
            for h in range(HEADS):
                parts[h, n * rows + i] = value[h]
    for step, out in enumerate((s0, s1, s2, s3)):
        out[...] = parts[lax.rem(y + step, 4)]


def project_call(group, cotangent, gain, shift, wq, wk, wv, wg, gate_bias, wo):
    rows = group.shape[0]
    sent = jax.ShapeDtypeStruct((4 * rows, HEAD_DIM, BLOCK), bf16)
    return pl.pallas_call(
        project_kernel,
        out_shape=(sent,) * 4 + (jax.ShapeDtypeStruct((rows, BLOCK, BLOCK), f32),),
        scratch_shapes=[pltpu.VMEM((HEADS, 4 * rows, HEAD_DIM, BLOCK), bf16)],
        compiler_params=pltpu.CompilerParams(vmem_limit_bytes=VMEM_LIMIT),
        cost_estimate=pl.CostEstimate(
            flops=110_000_000, bytes_accessed=2_000_000, transcendentals=100_000
        ),
        name="project",
    )(group, cotangent, gain, shift, wq, wk, wv, wg, gate_bias, wo)


def attention_kernel(
    mask_ref, bias_own, bias_other, s0, s1, s2, s3, kv_other,
    out_own, out_other, out_q, keep, send,
    bias, grad, key_t, value_t, key_s, value_s, query_t, up_t, key_out,
):
    x, zh, core, z, y = place()
    keys, queries = bias.shape
    rows = key_t.shape[0]

    for blk in range(keys // BLOCK):
        live = jnp.broadcast_to(mask_ref[blk : blk + 1, :].astype(f32), (BLOCK, BLOCK)).T
        bias[blk * BLOCK : (blk + 1) * BLOCK, :] = jnp.concatenate([live] * (queries // BLOCK), 1)
    for source, c in ((bias_own, core), (bias_other, 1 - core)):
        for dx in range(4):
            for dz in range(4):
                r = lax.rem(x - dx + 4, 4) * 8 + lax.rem(zh - dz + 4, 4) * 2 + c
                at = pl.ds(pl.multiple_of(r * 32, 32), 32)
                for dy in range(4):
                    lanes = slice(dy * BLOCK, (dy + 1) * BLOCK)
                    bias[at, lanes] = jnp.where(
                        bias[at, lanes] > 0.0, source[dx, dy, dz].astype(f32), -jnp.inf
                    )
    grad[...] = jnp.zeros_like(grad)

    for step, own in enumerate((s0, s1, s2, s3)):
        yy = lax.rem(y - step + 4, 4)
        for source, c in ((own, z * 4 + yy), (kv_other.at[step], (1 - z) * 4 + yy)):
            at = pl.ds(pl.multiple_of(c * BLOCK, BLOCK), BLOCK)
            for i in range(rows):
                k, v = source[i], source[rows + i]
                key_t[i, :, at] = k
                value_t[i, :, at] = v
                key_s[i, at, :] = k.astype(f32).T.astype(bf16)
                value_s[i, at, :] = v.astype(f32).T.astype(bf16)
        for i in range(rows):
            query_t[i, :, step * BLOCK : (step + 1) * BLOCK] = own[2 * rows + i]
            up_t[i, :, step * BLOCK : (step + 1) * BLOCK] = own[3 * rows + i]

    width = 256

    def row(i, carry):
        grad_key = jnp.zeros((keys, HEAD_DIM), f32)
        grad_value = jnp.zeros((keys, HEAD_DIM), f32)
        for part in range(queries // width):
            lanes = slice(part * width, (part + 1) * width)
            q, g = query_t[i, :, lanes], up_t[i, :, lanes]
            scores = jnp.dot(key_s[i], q, preferred_element_type=f32) + bias[:, lanes]
            raised = jnp.exp(scores)
            weights = raised * (1.0 / jnp.sum(raised, axis=0, keepdims=True))
            low = weights.astype(bf16)
            attended = jnp.dot(value_t[i], low, preferred_element_type=f32)
            delta = jnp.sum(g.astype(f32) * attended, axis=0, keepdims=True)
            grad_weights = jnp.dot(value_s[i], g, preferred_element_type=f32)
            grad_scores = weights * (grad_weights - delta)
            grad[:, lanes] += grad_scores
            scores_low = grad_scores.astype(bf16)
            grad_query = jnp.dot(key_t[i], scores_low, preferred_element_type=f32) * SCALE
            grad_key += lax.dot_general(scores_low, q, NT, preferred_element_type=f32)
            grad_value += lax.dot_general(low, g, NT, preferred_element_type=f32)
            for n in range(width // BLOCK):
                block, at = part * (width // BLOCK) + n, slice(n * BLOCK, (n + 1) * BLOCK)
                out_q[block, i] = grad_query[:, at].astype(bf16)
                out_q[block, rows + i] = attended[:, at].astype(bf16)
        both = jnp.concatenate([grad_key, grad_value], axis=1).T.astype(bf16)
        key_out[i, 0] = both[:HEAD_DIM]
        key_out[i, 1] = both[HEAD_DIM:]
        return carry

    lax.fori_loop(0, rows, row, 0)

    for step in range(4):
        yy = lax.rem(y - step + 4, 4)
        for out, c in ((out_own, z * 4 + yy), (out_other, (1 - z) * 4 + yy)):
            at = pl.ds(pl.multiple_of(c * BLOCK, BLOCK), BLOCK)
            for i in range(rows):
                out[step, i] = key_out[i, 0, :, at]
                out[step, rows + i] = key_out[i, 1, :, at]
    for out, c in ((keep, core), (send, 1 - core)):
        for dx in range(4):
            for dz in range(4):
                r = lax.rem(x - dx + 4, 4) * 8 + lax.rem(zh - dz + 4, 4) * 2 + c
                at = pl.ds(pl.multiple_of(r * 32, 32), 32)
                for dy in range(4):
                    out[dx, dz, dy] = grad[at, dy * BLOCK : (dy + 1) * BLOCK].astype(out.dtype)


def attention_call(mask, bias_own, bias_other, pieces, kv_other):
    rows = kv_other.shape[1] // 2
    keys = mask.shape[0] * mask.shape[1]
    queries = keys // 2
    part = jax.ShapeDtypeStruct(kv_other.shape, bf16)
    return pl.pallas_call(
        attention_kernel,
        out_shape=(
            part, part, part,
            jax.ShapeDtypeStruct(bias_own.shape, f32),
            jax.ShapeDtypeStruct(bias_own.shape, bf16),
        ),
        scratch_shapes=[
            pltpu.VMEM((keys, queries), f32),
            pltpu.VMEM((keys, queries), f32),
            pltpu.VMEM((rows, HEAD_DIM, keys), bf16),
            pltpu.VMEM((rows, HEAD_DIM, keys), bf16),
            pltpu.VMEM((rows, keys, HEAD_DIM), bf16),
            pltpu.VMEM((rows, keys, HEAD_DIM), bf16),
            pltpu.VMEM((rows, HEAD_DIM, queries), bf16),
            pltpu.VMEM((rows, HEAD_DIM, queries), bf16),
            pltpu.VMEM((rows, 2, HEAD_DIM, keys), bf16),
        ],
        compiler_params=pltpu.CompilerParams(vmem_limit_bytes=VMEM_LIMIT),
        cost_estimate=pl.CostEstimate(
            flops=8_000_000_000, bytes_accessed=6_000_000, transcendentals=2_700_000
        ),
        name="attention",
    )(mask, bias_own, bias_other, *pieces, kv_other)


def add_core_kernel(keep, came, k0, s1, s2, s3):
    for n, out in enumerate((k0, s1, s2, s3)):
        out[...] = (keep[n] + came[n].astype(f32)).astype(out.dtype)


def add_core(keep, came):
    shape = keep.shape[1:]
    return pl.pallas_call(
        add_core_kernel,
        out_shape=(jax.ShapeDtypeStruct(shape, f32),) + (jax.ShapeDtypeStruct(shape, bf16),) * 3,
        compiler_params=pltpu.CompilerParams(vmem_limit_bytes=VMEM_LIMIT),
        name="add_core",
    )(keep, came)


def add_four_kernel(keep, c1, c2, c3, k0, s1, s2, s3):
    for n, out in enumerate((k0, s1, s2, s3)):
        total = keep[n] + c1[n].astype(f32) + c2[n].astype(f32) + c3[n].astype(f32)
        out[...] = total.astype(out.dtype)


def add_four(keep, c1, c2, c3):
    shape = keep.shape[1:]
    return pl.pallas_call(
        add_four_kernel,
        out_shape=(jax.ShapeDtypeStruct(shape, f32),) + (jax.ShapeDtypeStruct(shape, bf16),) * 3,
        compiler_params=pltpu.CompilerParams(vmem_limit_bytes=VMEM_LIMIT),
        name="add_four",
    )(keep, c1, c2, c3)


def pack_kernel(keep, c1, c2, c3, own, came, query, t0, t1, t2, t3):
    half = own.shape[1]
    for n, out in enumerate((t0, t1, t2, t3)):
        out[:half] = (own[n].astype(f32) + came[n].astype(f32)).astype(bf16)
        out[half : 2 * half] = query[n]
        total = keep[n] + c1[n].astype(f32) + c2[n].astype(f32) + c3[n].astype(f32)
        out[2 * half] = total.astype(bf16)


def pack_call(keep, c1, c2, c3, own, came, query):
    half, *tile = own.shape[1:]
    return pl.pallas_call(
        pack_kernel,
        out_shape=(jax.ShapeDtypeStruct((2 * half + 1, *tile), bf16),) * 4,
        compiler_params=pltpu.CompilerParams(vmem_limit_bytes=VMEM_LIMIT),
        name="pack",
    )(keep, c1, c2, c3, own, came, query)


def group_kernel(
    group_ref, gain_ref, wq_ref, wk_ref, wv_ref, wg_ref, coef,
    t0, t1, t2, t3, out_ref,
):
    _, _, _, _, y = place()
    gain = gain_ref[...]
    turn = lax.rem(4 - y, 4) * HEAD_DIM
    wq, wk, wv, wg = (
        pltpu.roll(w[...].astype(f32), turn, 1).astype(bf16)
        for w in (wq_ref, wk_ref, wv_ref, wg_ref)
    )
    weights = jnp.concatenate([wk, wv, wq, wg, wg], axis=1)
    rows = group_ref.shape[0]
    for i in range(rows):
        parts = [[] for _ in range(5)]
        for step, t in enumerate((t0, t1, t2, t3)):
            h = lax.rem(y + step, 4)
            at = pl.multiple_of(h * HEAD_DIM, HEAD_DIM)
            gate = coef[i, pl.ds(at, HEAD_DIM), :] * t[3 * rows + i].astype(f32)
            high, low = split_high_low(gate)
            pieces = (t[i], t[rows + i], t[2 * rows + i], high, low)
            for part, piece in zip(parts, pieces):
                part.append(piece)
        stacked = jnp.concatenate(sum(parts, []), axis=0)
        upstream = jnp.dot(weights, stacked, preferred_element_type=f32).T
        x = group_ref[i].astype(f32)
        centered = x - jnp.mean(x, axis=-1, keepdims=True)
        reciprocal = lax.rsqrt(jnp.mean(centered * centered, axis=-1, keepdims=True) + EPS)
        normalized = centered * reciprocal
        scaled = upstream * gain
        first = jnp.mean(scaled, axis=-1, keepdims=True)
        second = jnp.mean(scaled * normalized, axis=-1, keepdims=True)
        out_ref[i] = (reciprocal * (scaled - first - normalized * second)).astype(bf16)


def group_call(group, gain, wq, wk, wv, wg, coef, pieces):
    return pl.pallas_call(
        group_kernel,
        out_shape=jax.ShapeDtypeStruct(group.shape, bf16),
        compiler_params=pltpu.CompilerParams(vmem_limit_bytes=VMEM_LIMIT),
        cost_estimate=pl.CostEstimate(
            flops=160_000_000, bytes_accessed=2_000_000, transcendentals=1000
        ),
        name="group_backward",
    )(group, gain, wq, wk, wv, wg, coef, *pieces)


def pair_kernel(pair_ref, gain_ref, weight_ref, t0, t1, t2, t3, out_ref, grad, db):
    _, _, _, _, y = place()
    weight = jnp.concatenate(
        [weight_ref[...].astype(f32), jnp.zeros((8 - HEADS, BLOCK), f32)], axis=0
    ) * gain_ref[...]
    weight = weight - jnp.mean(weight, axis=-1, keepdims=True)
    high, low = split_high_low(weight)
    weights = jnp.concatenate([high, high, low, jnp.zeros((8, BLOCK), bf16)], axis=0)
    db[...] = jnp.zeros_like(db)
    last = t0.shape[0] - 1
    for step, t in enumerate((t0, t1, t2, t3)):
        h = lax.rem(y + step, 4)
        value = t[last].astype(f32)
        for k in range(32):
            db[k, pl.ds(h, 1), :] = value[k : k + 1]

    for k in range(32):
        db_high, db_low = split_high_low(db[k])
        left = jnp.concatenate([db_high, db_low, db_high, jnp.zeros((8, BLOCK), bf16)], axis=0)
        grad[pl.ds(k, BLOCK, stride=32), :] = lax.dot_general(
            left, weights, TN, preferred_element_type=f32
        )

    def rows(step, carry):
        x = pair_ref[pl.ds(step * 16, 16)].astype(f32).reshape(512, BLOCK)
        centered = x - jnp.mean(x, axis=-1, keepdims=True)
        reciprocal = lax.rsqrt(jnp.mean(centered * centered, axis=-1, keepdims=True) + EPS)
        normalized = centered * reciprocal
        scaled = grad[pl.ds(pl.multiple_of(step * 512, 512), 512), :]
        second = jnp.mean(scaled * normalized, axis=-1, keepdims=True)
        result = reciprocal * (scaled - normalized * second)
        out_ref[pl.ds(step * 16, 16)] = result.astype(bf16).reshape(16, 32, BLOCK)
        return carry

    lax.fori_loop(0, 8, rows, 0)


def pair_call(pair, gain, weight, pieces):
    return pl.pallas_call(
        pair_kernel,
        out_shape=jax.ShapeDtypeStruct(pair.shape, bf16),
        scratch_shapes=[pltpu.VMEM((4096, BLOCK), f32), pltpu.VMEM((32, 8, BLOCK), f32)],
        compiler_params=pltpu.CompilerParams(vmem_limit_bytes=VMEM_LIMIT),
        cost_estimate=pl.CostEstimate(
            flops=60_000_000, bytes_accessed=2_200_000, transcendentals=4096
        ),
        name="pair_backward",
    )(pair, gain, weight, *pieces)


def along(value, axis, step):
    size = 2 if axis in ("core", "z") else 4
    return lax.ppermute(value, axis, [(p, (p + step) % size) for p in range(size)])


def per_device(
    group, pair, mask, ln_gain, ln_shift, w_query, w_key, w_value, w_gate, gate_bias, w_bias,
    w_out, cotangent,
):
    gain, shift = ln_gain.reshape(1, BLOCK), ln_shift.reshape(1, BLOCK)
    half = 2 * group.shape[0]
    bias = bias_call(pair, gain, shift, w_bias.T)
    bias, group, cotangent = lax.optimization_barrier((bias, group, cotangent))
    *sent, coef = project_call(
        group, cotangent, gain, shift, w_query, w_key, w_value, w_gate,
        gate_bias.reshape(1, BLOCK), w_out,
    )
    turned = turn_call([bias] + [along(bias, "zh", d) for d in range(1, 4)])
    pieces = [sent[0]] + [along(sent[d], "y", d) for d in range(1, 4)]
    turned, pieces = lax.optimization_barrier((turned, pieces))
    blocks = [turned[0]] + [along(turned[d], "y", d) for d in range(1, 4)]
    key_value = jnp.stack([p[:half] for p in pieces])
    near = jnp.stack(blocks)
    line, kv_other = lax.optimization_barrier(
        ([near] + [along(near, "x", d) for d in range(1, 4)], along(key_value, "z", 1))
    )
    plane = jnp.stack(line)
    other = along(plane, "core", 1)

    out_own, out_other, out_q, keep, send = attention_call(
        mask.reshape(-1, BLOCK), plane, other, pieces, kv_other
    )

    first = add_core(keep, along(send, "core", 1))
    came = along(out_other, "z", 1)
    second = add_four(first[0], *(along(first[d], "x", -d) for d in range(1, 4)))
    third = [along(second[d], "zh", -d) for d in range(1, 4)]
    packed = pack_call(second[0], *third, out_own, came, out_q)
    back = [packed[0]] + [along(packed[d], "y", -d) for d in range(1, 4)]

    grad_group = group_call(group, gain, w_query, w_key, w_value, w_gate, coef, back)
    grad_pair = pair_call(pair, gain, w_bias.T, back)
    return (grad_group, grad_pair)


def solution(mesh):
    fine = jax.sharding.Mesh(mesh.devices.reshape(4, 4, 2, 2, 4), ("x", "zh", "core", "z", "y"))
    row, col = ("x", "zh", "core"), ("z", "y")
    placed = (
        P(row, col, None),
        P(col, row, None),
        P(), P(), P(), P(), P(), P(), P(), P(), P(), P(),
        P(row, col, None),
    )
    return jax.shard_map(
        per_device,
        mesh=fine,
        in_specs=placed,
        out_specs=(P(row, col, None), P(col, row, None)),
        check_vma=False,
    )
```

```python
import jax
import jax.numpy as jnp
from jax import lax
from jax.experimental import pallas as pl
from jax.experimental.pallas import tpu as pltpu
from jax.sharding import PartitionSpec as P

HEADS = 4
HEAD_DIM = 32
BLOCK = 128
EPS = 1e-05
SCALE = HEAD_DIM ** (-0.5)
VMEM_LIMIT = 48 * 1024 * 1024

bf16, f32 = jnp.bfloat16, jnp.float32
NT = (((1,), (1,)), ((), ()))
TN = (((0,), (0,)), ((), ()))


def place():
    return tuple(lax.axis_index(name) for name in ("x", "zh", "core", "z", "y"))


def split_high_low(value):
    high = value.astype(bf16)
    return high, (value - high.astype(f32)).astype(bf16)


def bias_kernel(pair_ref, gain_ref, shift_ref, weight_ref, out_ref, normed, heads):
    gain, shift = gain_ref[...], shift_ref[...]
    weight_t = jnp.concatenate(
        [weight_ref[...].astype(f32), jnp.zeros((16 - HEADS, BLOCK), f32)], axis=0
    ).astype(bf16)

    def rows(step, carry):
        x = pair_ref[pl.ds(step * 16, 16)].astype(f32).reshape(512, BLOCK)
        centered = x - jnp.mean(x, axis=-1, keepdims=True)
        reciprocal = lax.rsqrt(jnp.mean(centered * centered, axis=-1, keepdims=True) + EPS)
        low = (centered * reciprocal * gain + shift).astype(bf16).astype(f32)
        normed[pl.ds(pl.multiple_of(step * 512, 512), 512), :] = low
        return carry

    lax.fori_loop(0, 8, rows, 0)

    for k in range(32):
        block = normed[pl.ds(k, BLOCK, stride=32), :].astype(bf16)
        product = lax.dot_general(weight_t, block, NT, preferred_element_type=f32)
        for h in range(HEADS):
            heads[h, k : k + 1, :] = product[h : h + 1]
    y = lax.axis_index("y")
    for step in range(HEADS):
        out_ref[step] = heads[lax.rem(y + step, 4)].astype(bf16)


def bias_call(pair, gain, shift, weight):
    return pl.pallas_call(
        bias_kernel,
        out_shape=jax.ShapeDtypeStruct((HEADS, 32, BLOCK), bf16),
        scratch_shapes=[pltpu.VMEM((4096, BLOCK), f32), pltpu.VMEM((HEADS, 32, BLOCK), f32)],
        compiler_params=pltpu.CompilerParams(vmem_limit_bytes=VMEM_LIMIT),
        cost_estimate=pl.CostEstimate(
            flops=3_500_000_000, bytes_accessed=1_200_000, transcendentals=4096
        ),
        name="pair_bias",
    )(pair, gain, shift, weight)


def turn_kernel(g0, g1, g2, g3, s0, s1, s2, s3):
    for n, source in enumerate((g0, g1, g2, g3)):
        for step, out in enumerate((s0, s1, s2, s3)):
            out[n] = source[step]


def turn_call(gathered):
    return pl.pallas_call(
        turn_kernel,
        out_shape=(jax.ShapeDtypeStruct(gathered[0].shape, bf16),) * 4,
        compiler_params=pltpu.CompilerParams(vmem_limit_bytes=VMEM_LIMIT),
        name="turn",
    )(*gathered)


def project_kernel(
    group_ref, cot_ref, gain_ref, shift_ref, wq_ref, wk_ref, wv_ref, wg_ref, gb_ref, wo_ref,
    s0, s1, s2, s3, coef, parts,
):
    y = lax.axis_index("y")
    gain, shift = gain_ref[...], shift_ref[...]
    gate_bias = jnp.broadcast_to(gb_ref[...], (BLOCK, BLOCK)).T
    turned = [w[...].astype(f32).T.astype(bf16) for w in (wq_ref, wk_ref, wv_ref, wg_ref)]
    rows = group_ref.shape[0]
    for i in range(rows):
        x = group_ref[i].astype(f32)
        centered = x - jnp.mean(x, axis=-1, keepdims=True)
        reciprocal = lax.rsqrt(jnp.mean(centered * centered, axis=-1, keepdims=True) + EPS)
        low = (centered * reciprocal * gain + shift).astype(bf16)
        dots = [lax.dot_general(w, low, NT, preferred_element_type=f32) for w in turned]
        gating = jax.nn.sigmoid(dots[3] + gate_bias)
        gated = lax.dot_general(wo_ref[...], cot_ref[i], NT, preferred_element_type=f32)
        upstream = gated * gating
        coef[i] = upstream * (1.0 - gating)
        for n, value in enumerate((dots[1], dots[2], dots[0] * SCALE, upstream)):
            value = value.astype(bf16).reshape(HEADS, HEAD_DIM, BLOCK)
            for h in range(HEADS):
                parts[h, n * rows + i] = value[h]
    for step, out in enumerate((s0, s1, s2, s3)):
        out[...] = parts[lax.rem(y + step, 4)]


def project_call(group, cotangent, gain, shift, wq, wk, wv, wg, gate_bias, wo):
    rows = group.shape[0]
    sent = jax.ShapeDtypeStruct((4 * rows, HEAD_DIM, BLOCK), bf16)
    return pl.pallas_call(
        project_kernel,
        out_shape=(sent,) * 4 + (jax.ShapeDtypeStruct((rows, BLOCK, BLOCK), f32),),
        scratch_shapes=[pltpu.VMEM((HEADS, 4 * rows, HEAD_DIM, BLOCK), bf16)],
        compiler_params=pltpu.CompilerParams(vmem_limit_bytes=VMEM_LIMIT),
        cost_estimate=pl.CostEstimate(
            flops=110_000_000, bytes_accessed=2_000_000, transcendentals=100_000
        ),
        name="project",
    )(group, cotangent, gain, shift, wq, wk, wv, wg, gate_bias, wo)


def attention_kernel(
    mask_ref, bias_own, bias_other, s0, s1, s2, s3, kv_other,
    out_own, out_other, out_q, keep, send,
    bias, grad, key_t, value_t, key_s, value_s, query_t, up_t, key_out,
):
    x, zh, core, z, y = place()
    keys, queries = bias.shape
    rows = key_t.shape[0]

    for blk in range(keys // BLOCK):
        live = jnp.broadcast_to(mask_ref[blk : blk + 1, :].astype(f32), (BLOCK, BLOCK)).T
        bias[blk * BLOCK : (blk + 1) * BLOCK, :] = jnp.concatenate([live] * (queries // BLOCK), 1)
    for source, c in ((bias_own, core), (bias_other, 1 - core)):
        for dx in range(4):
            for dz in range(4):
                r = lax.rem(x - dx + 4, 4) * 8 + lax.rem(zh - dz + 4, 4) * 2 + c
                at = pl.ds(pl.multiple_of(r * 32, 32), 32)
                for dy in range(4):
                    lanes = slice(dy * BLOCK, (dy + 1) * BLOCK)
                    bias[at, lanes] = jnp.where(
                        bias[at, lanes] > 0.0, source[dx, dy, dz].astype(f32), -jnp.inf
                    )
    grad[...] = jnp.zeros_like(grad)

    for step, own in enumerate((s0, s1, s2, s3)):
        yy = lax.rem(y - step + 4, 4)
        for source, c in ((own, z * 4 + yy), (kv_other.at[step], (1 - z) * 4 + yy)):
            at = pl.ds(pl.multiple_of(c * BLOCK, BLOCK), BLOCK)
            for i in range(rows):
                k, v = source[i], source[rows + i]
                key_t[i, :, at] = k
                value_t[i, :, at] = v
                key_s[i, at, :] = k.astype(f32).T.astype(bf16)
                value_s[i, at, :] = v.astype(f32).T.astype(bf16)
        for i in range(rows):
            query_t[i, :, step * BLOCK : (step + 1) * BLOCK] = own[2 * rows + i]
            up_t[i, :, step * BLOCK : (step + 1) * BLOCK] = own[3 * rows + i]

    width = 512

    def row(i, carry):
        grad_key = jnp.zeros((keys, HEAD_DIM), f32)
        grad_value = jnp.zeros((keys, HEAD_DIM), f32)
        for part in range(queries // width):
            lanes = slice(part * width, (part + 1) * width)
            q, g = query_t[i, :, lanes], up_t[i, :, lanes]
            scores = jnp.dot(key_s[i], q, preferred_element_type=f32) + bias[:, lanes]
            raised = jnp.exp(scores)
            weights = raised * (1.0 / jnp.sum(raised, axis=0, keepdims=True))
            low = weights.astype(bf16)
            attended = jnp.dot(value_t[i], low, preferred_element_type=f32)
            delta = jnp.sum(g.astype(f32) * attended, axis=0, keepdims=True)
            grad_weights = jnp.dot(value_s[i], g, preferred_element_type=f32)
            grad_scores = weights * (grad_weights - delta)
            grad[:, lanes] += grad_scores
            scores_low = grad_scores.astype(bf16)
            grad_query = jnp.dot(key_t[i], scores_low, preferred_element_type=f32) * SCALE
            grad_key += lax.dot_general(scores_low, q, NT, preferred_element_type=f32)
            grad_value += lax.dot_general(low, g, NT, preferred_element_type=f32)
            for n in range(width // BLOCK):
                block, at = part * (width // BLOCK) + n, slice(n * BLOCK, (n + 1) * BLOCK)
                out_q[block, i] = grad_query[:, at].astype(bf16)
                out_q[block, rows + i] = attended[:, at].astype(bf16)
        both = jnp.concatenate([grad_key, grad_value], axis=1).T.astype(bf16)
        key_out[i, 0] = both[:HEAD_DIM]
        key_out[i, 1] = both[HEAD_DIM:]
        return carry

    lax.fori_loop(0, rows, row, 0)

    for step in range(4):
        yy = lax.rem(y - step + 4, 4)
        for out, c in ((out_own, z * 4 + yy), (out_other, (1 - z) * 4 + yy)):
            at = pl.ds(pl.multiple_of(c * BLOCK, BLOCK), BLOCK)
            for i in range(rows):
                out[step, i] = key_out[i, 0, :, at]
                out[step, rows + i] = key_out[i, 1, :, at]
    for out, c in ((keep, core), (send, 1 - core)):
        for dx in range(4):
            for dz in range(4):
                r = lax.rem(x - dx + 4, 4) * 8 + lax.rem(zh - dz + 4, 4) * 2 + c
                at = pl.ds(pl.multiple_of(r * 32, 32), 32)
                for dy in range(4):
                    out[dx, dz, dy] = grad[at, dy * BLOCK : (dy + 1) * BLOCK].astype(out.dtype)


def attention_call(mask, bias_own, bias_other, pieces, kv_other):
    rows = kv_other.shape[1] // 2
    keys = mask.shape[0] * mask.shape[1]
    queries = keys // 2
    part = jax.ShapeDtypeStruct(kv_other.shape, bf16)
    return pl.pallas_call(
        attention_kernel,
        out_shape=(
            part, part, part,
            jax.ShapeDtypeStruct(bias_own.shape, f32),
            jax.ShapeDtypeStruct(bias_own.shape, bf16),
        ),
        scratch_shapes=[
            pltpu.VMEM((keys, queries), f32),
            pltpu.VMEM((keys, queries), f32),
            pltpu.VMEM((rows, HEAD_DIM, keys), bf16),
            pltpu.VMEM((rows, HEAD_DIM, keys), bf16),
            pltpu.VMEM((rows, keys, HEAD_DIM), bf16),
            pltpu.VMEM((rows, keys, HEAD_DIM), bf16),
            pltpu.VMEM((rows, HEAD_DIM, queries), bf16),
            pltpu.VMEM((rows, HEAD_DIM, queries), bf16),
            pltpu.VMEM((rows, 2, HEAD_DIM, keys), bf16),
        ],
        compiler_params=pltpu.CompilerParams(vmem_limit_bytes=VMEM_LIMIT),
        cost_estimate=pl.CostEstimate(
            flops=8_000_000_000, bytes_accessed=6_000_000, transcendentals=2_700_000
        ),
        name="attention",
    )(mask, bias_own, bias_other, *pieces, kv_other)


def add_core_kernel(keep, came, k0, s1, s2, s3):
    for n, out in enumerate((k0, s1, s2, s3)):
        out[...] = (keep[n] + came[n].astype(f32)).astype(out.dtype)


def add_core(keep, came):
    shape = keep.shape[1:]
    return pl.pallas_call(
        add_core_kernel,
        out_shape=(jax.ShapeDtypeStruct(shape, f32),) + (jax.ShapeDtypeStruct(shape, bf16),) * 3,
        compiler_params=pltpu.CompilerParams(vmem_limit_bytes=VMEM_LIMIT),
        name="add_core",
    )(keep, came)


def add_four_kernel(keep, c1, c2, c3, k0, s1, s2, s3):
    for n, out in enumerate((k0, s1, s2, s3)):
        total = keep[n] + c1[n].astype(f32) + c2[n].astype(f32) + c3[n].astype(f32)
        out[...] = total.astype(out.dtype)


def add_four(keep, c1, c2, c3):
    shape = keep.shape[1:]
    return pl.pallas_call(
        add_four_kernel,
        out_shape=(jax.ShapeDtypeStruct(shape, f32),) + (jax.ShapeDtypeStruct(shape, bf16),) * 3,
        compiler_params=pltpu.CompilerParams(vmem_limit_bytes=VMEM_LIMIT),
        name="add_four",
    )(keep, c1, c2, c3)


def add_last_kernel(keep, c1, c2, c3, s0, s1, s2, s3):
    for n, out in enumerate((s0, s1, s2, s3)):
        total = keep[n] + c1[n].astype(f32) + c2[n].astype(f32) + c3[n].astype(f32)
        out[...] = total.astype(bf16)


def add_last(keep, c1, c2, c3):
    return pl.pallas_call(
        add_last_kernel,
        out_shape=(jax.ShapeDtypeStruct(keep.shape[1:], bf16),) * 4,
        compiler_params=pltpu.CompilerParams(vmem_limit_bytes=VMEM_LIMIT),
        name="add_last",
    )(keep, c1, c2, c3)


def pack_kernel(own, came, query, t0, t1, t2, t3):
    half = own.shape[1]
    for n, out in enumerate((t0, t1, t2, t3)):
        out[:half] = (own[n].astype(f32) + came[n].astype(f32)).astype(bf16)
        out[half:] = query[n]


def pack_call(own, came, query):
    half, *tile = own.shape[1:]
    return pl.pallas_call(
        pack_kernel,
        out_shape=(jax.ShapeDtypeStruct((2 * half, *tile), bf16),) * 4,
        compiler_params=pltpu.CompilerParams(vmem_limit_bytes=VMEM_LIMIT),
        name="pack",
    )(own, came, query)


def group_kernel(
    group_ref, gain_ref, wq_ref, wk_ref, wv_ref, wg_ref, coef,
    t0, t1, t2, t3, out_ref,
):
    _, _, _, _, y = place()
    gain = gain_ref[...]
    turn = lax.rem(4 - y, 4) * HEAD_DIM
    wq, wk, wv, wg = (
        pltpu.roll(w[...].astype(f32), turn, 1).astype(bf16)
        for w in (wq_ref, wk_ref, wv_ref, wg_ref)
    )
    weights = jnp.concatenate([wk, wv, wq, wg, wg], axis=1)
    rows = group_ref.shape[0]
    for i in range(rows):
        parts = [[] for _ in range(5)]
        for step, t in enumerate((t0, t1, t2, t3)):
            h = lax.rem(y + step, 4)
            at = pl.multiple_of(h * HEAD_DIM, HEAD_DIM)
            gate = coef[i, pl.ds(at, HEAD_DIM), :] * t[3 * rows + i].astype(f32)
            high, low = split_high_low(gate)
            pieces = (t[i], t[rows + i], t[2 * rows + i], high, low)
            for part, piece in zip(parts, pieces):
                part.append(piece)
        stacked = jnp.concatenate(sum(parts, []), axis=0)
        upstream = jnp.dot(weights, stacked, preferred_element_type=f32).T
        x = group_ref[i].astype(f32)
        centered = x - jnp.mean(x, axis=-1, keepdims=True)
        reciprocal = lax.rsqrt(jnp.mean(centered * centered, axis=-1, keepdims=True) + EPS)
        normalized = centered * reciprocal
        scaled = upstream * gain
        first = jnp.mean(scaled, axis=-1, keepdims=True)
        second = jnp.mean(scaled * normalized, axis=-1, keepdims=True)
        out_ref[i] = (reciprocal * (scaled - first - normalized * second)).astype(bf16)


def group_call(group, gain, wq, wk, wv, wg, coef, pieces):
    return pl.pallas_call(
        group_kernel,
        out_shape=jax.ShapeDtypeStruct(group.shape, bf16),
        compiler_params=pltpu.CompilerParams(vmem_limit_bytes=VMEM_LIMIT),
        cost_estimate=pl.CostEstimate(
            flops=160_000_000, bytes_accessed=2_000_000, transcendentals=1000
        ),
        name="group_backward",
    )(group, gain, wq, wk, wv, wg, coef, *pieces)


def stats_kernel(pair_ref, xhat, recip):
    def rows(step, carry):
        x = pair_ref[pl.ds(step * 16, 16)].astype(f32).reshape(512, BLOCK)
        centered = x - jnp.mean(x, axis=-1, keepdims=True)
        reciprocal = lax.rsqrt(jnp.mean(centered * centered, axis=-1, keepdims=True) + EPS)
        at = pl.ds(pl.multiple_of(step * 512, 512), 512)
        xhat[at, :] = centered * reciprocal
        recip[at, :] = jnp.broadcast_to(reciprocal, (512, BLOCK))
        return carry

    lax.fori_loop(0, 8, rows, 0)


def stats_call(pair):
    return pl.pallas_call(
        stats_kernel,
        out_shape=(jax.ShapeDtypeStruct((4096, BLOCK), f32),) * 2,
        compiler_params=pltpu.CompilerParams(vmem_limit_bytes=VMEM_LIMIT),
        cost_estimate=pl.CostEstimate(
            flops=10_000_000, bytes_accessed=5_000_000, transcendentals=4096
        ),
        name="pair_stats",
    )(pair)


def pair_kernel(xhat, recip, gain_ref, weight_ref, t0, t1, t2, t3, out_ref, grad, db):
    y = lax.axis_index("y")
    weight = jnp.concatenate(
        [weight_ref[...].astype(f32), jnp.zeros((8 - HEADS, BLOCK), f32)], axis=0
    ) * gain_ref[...]
    weight = weight - jnp.mean(weight, axis=-1, keepdims=True)
    high, low = split_high_low(weight)
    weights = jnp.concatenate([high, high, low, jnp.zeros((8, BLOCK), bf16)], axis=0)
    db[...] = jnp.zeros_like(db)
    for step, t in enumerate((t0, t1, t2, t3)):
        h = lax.rem(y + step, 4)
        value = t[...].astype(f32)
        for k in range(32):
            db[k, pl.ds(h, 1), :] = value[k : k + 1]

    for k in range(32):
        db_high, db_low = split_high_low(db[k])
        left = jnp.concatenate([db_high, db_low, db_high, jnp.zeros((8, BLOCK), bf16)], axis=0)
        grad[pl.ds(k, BLOCK, stride=32), :] = lax.dot_general(
            left, weights, TN, preferred_element_type=f32
        )

    def rows(step, carry):
        at = pl.ds(pl.multiple_of(step * 512, 512), 512)
        scaled, normalized = grad[at, :], xhat[at, :]
        second = jnp.mean(scaled * normalized, axis=-1, keepdims=True)
        result = recip[at, :] * (scaled - normalized * second)
        out_ref[pl.ds(step * 16, 16)] = result.astype(bf16).reshape(16, 32, BLOCK)
        return carry

    lax.fori_loop(0, 8, rows, 0)


def pair_call(shape, stats, gain, weight, pieces):
    return pl.pallas_call(
        pair_kernel,
        out_shape=jax.ShapeDtypeStruct(shape, bf16),
        scratch_shapes=[pltpu.VMEM((4096, BLOCK), f32), pltpu.VMEM((32, 8, BLOCK), f32)],
        compiler_params=pltpu.CompilerParams(vmem_limit_bytes=VMEM_LIMIT),
        cost_estimate=pl.CostEstimate(
            flops=60_000_000, bytes_accessed=5_200_000, transcendentals=0
        ),
        name="pair_backward",
    )(*stats, gain, weight, *pieces)


def along(value, axis, step):
    size = 2 if axis in ("core", "z") else 4
    return lax.ppermute(value, axis, [(p, (p + step) % size) for p in range(size)])


def per_device(
    group, pair, mask, ln_gain, ln_shift, w_query, w_key, w_value, w_gate, gate_bias, w_bias,
    w_out, cotangent,
):
    gain, shift = ln_gain.reshape(1, BLOCK), ln_shift.reshape(1, BLOCK)
    half = 2 * group.shape[0]
    bias = bias_call(pair, gain, shift, w_bias.T)
    bias, group, cotangent = lax.optimization_barrier((bias, group, cotangent))
    *sent, coef = project_call(
        group, cotangent, gain, shift, w_query, w_key, w_value, w_gate,
        gate_bias.reshape(1, BLOCK), w_out,
    )
    turned = turn_call([bias] + [along(bias, "zh", d) for d in range(1, 4)])
    pieces = [sent[0]] + [along(sent[d], "y", d) for d in range(1, 4)]
    turned, pieces = lax.optimization_barrier((turned, pieces))
    blocks = [turned[0]] + [along(turned[d], "y", d) for d in range(1, 4)]
    key_value = jnp.stack([p[:half] for p in pieces])
    near = jnp.stack(blocks)
    line, kv_other = lax.optimization_barrier(
        ([near] + [along(near, "x", d) for d in range(1, 4)], along(key_value, "z", 1))
    )
    plane = jnp.stack(line)
    other = along(plane, "core", 1)

    out_own, out_other, out_q, keep, send = attention_call(
        mask.reshape(-1, BLOCK), plane, other, pieces, kv_other
    )

    first = add_core(keep, along(send, "core", 1))
    came = along(out_other, "z", 1)
    sums = [along(first[d], "x", -d) for d in range(1, 4)]
    packed = pack_call(out_own, came, out_q)
    sums, packed = lax.optimization_barrier((sums, packed))
    second = add_four(first[0], *sums)
    back = [packed[0]] + [along(packed[d], "y", -d) for d in range(1, 4)]
    third = [along(second[d], "zh", -d) for d in range(1, 4)]
    third, back = lax.optimization_barrier((third, back))
    last = add_last(second[0], *third)
    last = [last[0]] + [along(last[d], "y", -d) for d in range(1, 4)]

    grad_group = group_call(group, gain, w_query, w_key, w_value, w_gate, coef, back)
    grad_pair = pair_call(pair.shape, stats_call(pair), gain, w_bias.T, last)
    return (grad_group, grad_pair)


def solution(mesh):
    fine = jax.sharding.Mesh(mesh.devices.reshape(4, 4, 2, 2, 4), ("x", "zh", "core", "z", "y"))
    row, col = ("x", "zh", "core"), ("z", "y")
    placed = (
        P(row, col, None),
        P(col, row, None),
        P(), P(), P(), P(), P(), P(), P(), P(), P(), P(),
        P(row, col, None),
    )
    return jax.shard_map(
        per_device,
        mesh=fine,
        in_specs=placed,
        out_specs=(P(row, col, None), P(col, row, None)),
        check_vma=False,
    )
```

```python
import jax
import jax.numpy as jnp
from jax import lax
from jax.experimental import pallas as pl
from jax.experimental.pallas import tpu as pltpu
from jax.sharding import PartitionSpec as P

HEADS = 4
HEAD_DIM = 32
BLOCK = 128
EPS = 1e-05
SCALE = HEAD_DIM ** (-0.5)
VMEM_LIMIT = 48 * 1024 * 1024

bf16, f32 = jnp.bfloat16, jnp.float32
NT = (((1,), (1,)), ((), ()))
TN = (((0,), (0,)), ((), ()))


def place():
    return tuple(lax.axis_index(name) for name in ("x", "zh", "core", "z", "y"))


def split_high_low(value):
    high = value.astype(bf16)
    return high, (value - high.astype(f32)).astype(bf16)


def bias_kernel(pair_ref, gain_ref, shift_ref, weight_ref, out_ref, normed, heads):
    gain, shift = gain_ref[...], shift_ref[...]
    weight_t = jnp.concatenate(
        [weight_ref[...].astype(f32), jnp.zeros((16 - HEADS, BLOCK), f32)], axis=0
    ).astype(bf16)

    def rows(step, carry):
        x = pair_ref[pl.ds(step * 16, 16)].astype(f32).reshape(512, BLOCK)
        centered = x - jnp.mean(x, axis=-1, keepdims=True)
        reciprocal = lax.rsqrt(jnp.mean(centered * centered, axis=-1, keepdims=True) + EPS)
        low = (centered * reciprocal * gain + shift).astype(bf16).astype(f32)
        normed[pl.ds(pl.multiple_of(step * 512, 512), 512), :] = low
        return carry

    lax.fori_loop(0, 8, rows, 0)

    for k in range(32):
        block = normed[pl.ds(k, BLOCK, stride=32), :].astype(bf16)
        product = lax.dot_general(weight_t, block, NT, preferred_element_type=f32)
        for h in range(HEADS):
            heads[h, k : k + 1, :] = product[h : h + 1]
    y = lax.axis_index("y")
    for step in range(HEADS):
        out_ref[step] = heads[lax.rem(y + step, 4)].astype(bf16)


def bias_call(pair, gain, shift, weight):
    return pl.pallas_call(
        bias_kernel,
        out_shape=jax.ShapeDtypeStruct((HEADS, 32, BLOCK), bf16),
        scratch_shapes=[pltpu.VMEM((4096, BLOCK), f32), pltpu.VMEM((HEADS, 32, BLOCK), f32)],
        compiler_params=pltpu.CompilerParams(vmem_limit_bytes=VMEM_LIMIT),
        cost_estimate=pl.CostEstimate(
            flops=3_500_000_000, bytes_accessed=1_200_000, transcendentals=4096
        ),
        name="pair_bias",
    )(pair, gain, shift, weight)


def turn_kernel(g0, g1, g2, g3, s0, s1, s2, s3):
    for n, source in enumerate((g0, g1, g2, g3)):
        for step, out in enumerate((s0, s1, s2, s3)):
            out[n] = source[step]


def turn_call(gathered):
    return pl.pallas_call(
        turn_kernel,
        out_shape=(jax.ShapeDtypeStruct(gathered[0].shape, bf16),) * 4,
        compiler_params=pltpu.CompilerParams(vmem_limit_bytes=VMEM_LIMIT),
        name="turn",
    )(*gathered)


def project_kernel(
    group_ref, cot_ref, gain_ref, shift_ref, wq_ref, wk_ref, wv_ref, wg_ref, gb_ref, wo_ref,
    s0, s1, s2, s3, coef, parts,
):
    y = lax.axis_index("y")
    gain, shift = gain_ref[...], shift_ref[...]
    gate_bias = jnp.broadcast_to(gb_ref[...], (BLOCK, BLOCK)).T
    turned = [w[...].astype(f32).T.astype(bf16) for w in (wq_ref, wk_ref, wv_ref, wg_ref)]
    rows = group_ref.shape[0]
    for i in range(rows):
        x = group_ref[i].astype(f32)
        centered = x - jnp.mean(x, axis=-1, keepdims=True)
        reciprocal = lax.rsqrt(jnp.mean(centered * centered, axis=-1, keepdims=True) + EPS)
        low = (centered * reciprocal * gain + shift).astype(bf16)
        dots = [lax.dot_general(w, low, NT, preferred_element_type=f32) for w in turned]
        gating = jax.nn.sigmoid(dots[3] + gate_bias)
        gated = lax.dot_general(wo_ref[...], cot_ref[i], NT, preferred_element_type=f32)
        upstream = gated * gating
        coef[i] = upstream * (1.0 - gating)
        for n, value in enumerate((dots[1], dots[2], dots[0] * SCALE, upstream)):
            value = value.astype(bf16).reshape(HEADS, HEAD_DIM, BLOCK)
            for h in range(HEADS):
                parts[h, n * rows + i] = value[h]
    for step, out in enumerate((s0, s1, s2, s3)):
        out[...] = parts[lax.rem(y + step, 4)]


def project_call(group, cotangent, gain, shift, wq, wk, wv, wg, gate_bias, wo):
    rows = group.shape[0]
    sent = jax.ShapeDtypeStruct((4 * rows, HEAD_DIM, BLOCK), bf16)
    return pl.pallas_call(
        project_kernel,
        out_shape=(sent,) * 4 + (jax.ShapeDtypeStruct((rows, BLOCK, BLOCK), f32),),
        scratch_shapes=[pltpu.VMEM((HEADS, 4 * rows, HEAD_DIM, BLOCK), bf16)],
        compiler_params=pltpu.CompilerParams(vmem_limit_bytes=VMEM_LIMIT),
        cost_estimate=pl.CostEstimate(
            flops=110_000_000, bytes_accessed=2_000_000, transcendentals=100_000
        ),
        name="project",
    )(group, cotangent, gain, shift, wq, wk, wv, wg, gate_bias, wo)


def attention_kernel(
    mask_ref, bias_own, bias_other, s0, s1, s2, s3, kv_other,
    out_own, out_other, out_q, keep, send,
    bias, grad, key_t, value_t, key_s, value_s, query_t, up_t, key_out,
):
    x, zh, core, z, y = place()
    keys, queries = bias.shape
    rows = key_t.shape[0]

    for blk in range(keys // BLOCK):
        live = jnp.broadcast_to(mask_ref[blk : blk + 1, :].astype(f32), (BLOCK, BLOCK)).T
        bias[blk * BLOCK : (blk + 1) * BLOCK, :] = jnp.concatenate([live] * (queries // BLOCK), 1)
    for source, c in ((bias_own, core), (bias_other, 1 - core)):
        for dx in range(4):
            for dz in range(4):
                r = lax.rem(x - dx + 4, 4) * 8 + lax.rem(zh - dz + 4, 4) * 2 + c
                at = pl.ds(pl.multiple_of(r * 32, 32), 32)
                for dy in range(4):
                    lanes = slice(dy * BLOCK, (dy + 1) * BLOCK)
                    bias[at, lanes] = jnp.where(
                        bias[at, lanes] > 0.0, source[dx, dy, dz].astype(f32), -jnp.inf
                    )
    grad[...] = jnp.zeros_like(grad)

    for step, own in enumerate((s0, s1, s2, s3)):
        yy = lax.rem(y - step + 4, 4)
        for source, c in ((own, z * 4 + yy), (kv_other.at[step], (1 - z) * 4 + yy)):
            at = pl.ds(pl.multiple_of(c * BLOCK, BLOCK), BLOCK)
            for i in range(rows):
                k, v = source[i], source[rows + i]
                key_t[i, :, at] = k
                value_t[i, :, at] = v
                key_s[i, at, :] = k.astype(f32).T.astype(bf16)
                value_s[i, at, :] = v.astype(f32).T.astype(bf16)
        for i in range(rows):
            query_t[i, :, step * BLOCK : (step + 1) * BLOCK] = own[2 * rows + i]
            up_t[i, :, step * BLOCK : (step + 1) * BLOCK] = own[3 * rows + i]

    width = 512

    def row(i, carry):
        grad_key = jnp.zeros((keys, HEAD_DIM), f32)
        grad_value = jnp.zeros((keys, HEAD_DIM), f32)
        for part in range(queries // width):
            lanes = slice(part * width, (part + 1) * width)
            q, g = query_t[i, :, lanes], up_t[i, :, lanes]
            scores = jnp.dot(key_s[i], q, preferred_element_type=f32) + bias[:, lanes]
            raised = jnp.exp(scores)
            weights = raised * (1.0 / jnp.sum(raised, axis=0, keepdims=True))
            low = weights.astype(bf16)
            attended = jnp.dot(value_t[i], low, preferred_element_type=f32)
            delta = jnp.sum(g.astype(f32) * attended, axis=0, keepdims=True)
            grad_weights = jnp.dot(value_s[i], g, preferred_element_type=f32)
            grad_scores = weights * (grad_weights - delta)
            grad[:, lanes] += grad_scores
            scores_low = grad_scores.astype(bf16)
            grad_query = jnp.dot(key_t[i], scores_low, preferred_element_type=f32) * SCALE
            grad_key += lax.dot_general(scores_low, q, NT, preferred_element_type=f32)
            grad_value += lax.dot_general(low, g, NT, preferred_element_type=f32)
            for n in range(width // BLOCK):
                block, at = part * (width // BLOCK) + n, slice(n * BLOCK, (n + 1) * BLOCK)
                out_q[block, i] = grad_query[:, at].astype(bf16)
                out_q[block, rows + i] = attended[:, at].astype(bf16)
        both = jnp.concatenate([grad_key, grad_value], axis=1).T.astype(bf16)
        key_out[i, 0] = both[:HEAD_DIM]
        key_out[i, 1] = both[HEAD_DIM:]
        return carry

    for i in range(rows):
        row(i, 0)

    for step in range(4):
        yy = lax.rem(y - step + 4, 4)
        for out, c in ((out_own, z * 4 + yy), (out_other, (1 - z) * 4 + yy)):
            at = pl.ds(pl.multiple_of(c * BLOCK, BLOCK), BLOCK)
            for i in range(rows):
                out[step, i] = key_out[i, 0, :, at]
                out[step, rows + i] = key_out[i, 1, :, at]
    for out, c in ((keep, core), (send, 1 - core)):
        for dx in range(4):
            for dz in range(4):
                r = lax.rem(x - dx + 4, 4) * 8 + lax.rem(zh - dz + 4, 4) * 2 + c
                at = pl.ds(pl.multiple_of(r * 32, 32), 32)
                for dy in range(4):
                    out[dx, dz, dy] = grad[at, dy * BLOCK : (dy + 1) * BLOCK].astype(out.dtype)


def attention_call(mask, bias_own, bias_other, pieces, kv_other):
    rows = kv_other.shape[1] // 2
    keys = mask.shape[0] * mask.shape[1]
    queries = keys // 2
    part = jax.ShapeDtypeStruct(kv_other.shape, bf16)
    return pl.pallas_call(
        attention_kernel,
        out_shape=(
            part, part, part,
            jax.ShapeDtypeStruct(bias_own.shape, f32),
            jax.ShapeDtypeStruct(bias_own.shape, bf16),
        ),
        scratch_shapes=[
            pltpu.VMEM((keys, queries), f32),
            pltpu.VMEM((keys, queries), f32),
            pltpu.VMEM((rows, HEAD_DIM, keys), bf16),
            pltpu.VMEM((rows, HEAD_DIM, keys), bf16),
            pltpu.VMEM((rows, keys, HEAD_DIM), bf16),
            pltpu.VMEM((rows, keys, HEAD_DIM), bf16),
            pltpu.VMEM((rows, HEAD_DIM, queries), bf16),
            pltpu.VMEM((rows, HEAD_DIM, queries), bf16),
            pltpu.VMEM((rows, 2, HEAD_DIM, keys), bf16),
        ],
        compiler_params=pltpu.CompilerParams(vmem_limit_bytes=VMEM_LIMIT),
        cost_estimate=pl.CostEstimate(
            flops=8_000_000_000, bytes_accessed=6_000_000, transcendentals=2_700_000
        ),
        name="attention",
    )(mask, bias_own, bias_other, *pieces, kv_other)


def add_core_kernel(keep, came, k0, s1, s2, s3):
    for n, out in enumerate((k0, s1, s2, s3)):
        out[...] = (keep[n] + came[n].astype(f32)).astype(out.dtype)


def add_core(keep, came):
    shape = keep.shape[1:]
    return pl.pallas_call(
        add_core_kernel,
        out_shape=(jax.ShapeDtypeStruct(shape, f32),) + (jax.ShapeDtypeStruct(shape, bf16),) * 3,
        compiler_params=pltpu.CompilerParams(vmem_limit_bytes=VMEM_LIMIT),
        name="add_core",
    )(keep, came)


def add_four_kernel(keep, c1, c2, c3, k0, s1, s2, s3):
    for n, out in enumerate((k0, s1, s2, s3)):
        total = keep[n] + c1[n].astype(f32) + c2[n].astype(f32) + c3[n].astype(f32)
        out[...] = total.astype(out.dtype)


def add_four(keep, c1, c2, c3):
    shape = keep.shape[1:]
    return pl.pallas_call(
        add_four_kernel,
        out_shape=(jax.ShapeDtypeStruct(shape, f32),) + (jax.ShapeDtypeStruct(shape, bf16),) * 3,
        compiler_params=pltpu.CompilerParams(vmem_limit_bytes=VMEM_LIMIT),
        name="add_four",
    )(keep, c1, c2, c3)


def add_last_kernel(keep, c1, c2, c3, s0, s1, s2, s3):
    for n, out in enumerate((s0, s1, s2, s3)):
        total = keep[n] + c1[n].astype(f32) + c2[n].astype(f32) + c3[n].astype(f32)
        out[...] = total.astype(bf16)


def add_last(keep, c1, c2, c3):
    return pl.pallas_call(
        add_last_kernel,
        out_shape=(jax.ShapeDtypeStruct(keep.shape[1:], bf16),) * 4,
        compiler_params=pltpu.CompilerParams(vmem_limit_bytes=VMEM_LIMIT),
        name="add_last",
    )(keep, c1, c2, c3)


def pack_kernel(own, came, query, t0, t1, t2, t3):
    half = own.shape[1]
    for n, out in enumerate((t0, t1, t2, t3)):
        out[:half] = (own[n].astype(f32) + came[n].astype(f32)).astype(bf16)
        out[half:] = query[n]


def pack_call(own, came, query):
    half, *tile = own.shape[1:]
    return pl.pallas_call(
        pack_kernel,
        out_shape=(jax.ShapeDtypeStruct((2 * half, *tile), bf16),) * 4,
        compiler_params=pltpu.CompilerParams(vmem_limit_bytes=VMEM_LIMIT),
        name="pack",
    )(own, came, query)


def group_kernel(
    group_ref, gain_ref, wq_ref, wk_ref, wv_ref, wg_ref, coef,
    t0, t1, t2, t3, out_ref,
):
    _, _, _, _, y = place()
    gain = gain_ref[...]
    turn = lax.rem(4 - y, 4) * HEAD_DIM
    wq, wk, wv, wg = (
        pltpu.roll(w[...].astype(f32), turn, 1).astype(bf16)
        for w in (wq_ref, wk_ref, wv_ref, wg_ref)
    )
    weights = jnp.concatenate([wk, wv, wq, wg, wg], axis=1)
    rows = group_ref.shape[0]
    for i in range(rows):
        parts = [[] for _ in range(5)]
        for step, t in enumerate((t0, t1, t2, t3)):
            h = lax.rem(y + step, 4)
            at = pl.multiple_of(h * HEAD_DIM, HEAD_DIM)
            gate = coef[i, pl.ds(at, HEAD_DIM), :] * t[3 * rows + i].astype(f32)
            high, low = split_high_low(gate)
            pieces = (t[i], t[rows + i], t[2 * rows + i], high, low)
            for part, piece in zip(parts, pieces):
                part.append(piece)
        stacked = jnp.concatenate(sum(parts, []), axis=0)
        upstream = jnp.dot(weights, stacked, preferred_element_type=f32).T
        x = group_ref[i].astype(f32)
        centered = x - jnp.mean(x, axis=-1, keepdims=True)
        reciprocal = lax.rsqrt(jnp.mean(centered * centered, axis=-1, keepdims=True) + EPS)
        normalized = centered * reciprocal
        scaled = upstream * gain
        first = jnp.mean(scaled, axis=-1, keepdims=True)
        second = jnp.mean(scaled * normalized, axis=-1, keepdims=True)
        out_ref[i] = (reciprocal * (scaled - first - normalized * second)).astype(bf16)


def group_call(group, gain, wq, wk, wv, wg, coef, pieces):
    return pl.pallas_call(
        group_kernel,
        out_shape=jax.ShapeDtypeStruct(group.shape, bf16),
        compiler_params=pltpu.CompilerParams(vmem_limit_bytes=VMEM_LIMIT),
        cost_estimate=pl.CostEstimate(
            flops=160_000_000, bytes_accessed=2_000_000, transcendentals=1000
        ),
        name="group_backward",
    )(group, gain, wq, wk, wv, wg, coef, *pieces)


def stats_kernel(pair_ref, xhat, recip):
    def rows(step, carry):
        x = pair_ref[pl.ds(step * 16, 16)].astype(f32).reshape(512, BLOCK)
        centered = x - jnp.mean(x, axis=-1, keepdims=True)
        reciprocal = lax.rsqrt(jnp.mean(centered * centered, axis=-1, keepdims=True) + EPS)
        at = pl.ds(pl.multiple_of(step * 512, 512), 512)
        xhat[at, :] = centered * reciprocal
        recip[at, :] = jnp.broadcast_to(reciprocal, (512, BLOCK))
        return carry

    lax.fori_loop(0, 8, rows, 0)


def stats_call(pair):
    return pl.pallas_call(
        stats_kernel,
        out_shape=(jax.ShapeDtypeStruct((4096, BLOCK), f32),) * 2,
        compiler_params=pltpu.CompilerParams(vmem_limit_bytes=VMEM_LIMIT),
        cost_estimate=pl.CostEstimate(
            flops=10_000_000, bytes_accessed=5_000_000, transcendentals=4096
        ),
        name="pair_stats",
    )(pair)


def pair_kernel(xhat, recip, gain_ref, weight_ref, t0, t1, t2, t3, out_ref, grad, db):
    y = lax.axis_index("y")
    weight = jnp.concatenate(
        [weight_ref[...].astype(f32), jnp.zeros((8 - HEADS, BLOCK), f32)], axis=0
    ) * gain_ref[...]
    weight = weight - jnp.mean(weight, axis=-1, keepdims=True)
    high, low = split_high_low(weight)
    weights = jnp.concatenate([high, high, low, jnp.zeros((8, BLOCK), bf16)], axis=0)
    db[...] = jnp.zeros_like(db)
    for step, t in enumerate((t0, t1, t2, t3)):
        h = lax.rem(y + step, 4)
        value = t[...].astype(f32)
        for k in range(32):
            db[k, pl.ds(h, 1), :] = value[k : k + 1]

    for k in range(32):
        db_high, db_low = split_high_low(db[k])
        left = jnp.concatenate([db_high, db_low, db_high, jnp.zeros((8, BLOCK), bf16)], axis=0)
        grad[pl.ds(k, BLOCK, stride=32), :] = lax.dot_general(
            left, weights, TN, preferred_element_type=f32
        )

    def rows(step, carry):
        at = pl.ds(pl.multiple_of(step * 512, 512), 512)
        scaled, normalized = grad[at, :], xhat[at, :]
        second = jnp.mean(scaled * normalized, axis=-1, keepdims=True)
        result = recip[at, :] * (scaled - normalized * second)
        out_ref[pl.ds(step * 16, 16)] = result.astype(bf16).reshape(16, 32, BLOCK)
        return carry

    lax.fori_loop(0, 8, rows, 0)


def pair_call(shape, stats, gain, weight, pieces):
    return pl.pallas_call(
        pair_kernel,
        out_shape=jax.ShapeDtypeStruct(shape, bf16),
        scratch_shapes=[pltpu.VMEM((4096, BLOCK), f32), pltpu.VMEM((32, 8, BLOCK), f32)],
        compiler_params=pltpu.CompilerParams(vmem_limit_bytes=VMEM_LIMIT),
        cost_estimate=pl.CostEstimate(
            flops=60_000_000, bytes_accessed=5_200_000, transcendentals=0
        ),
        name="pair_backward",
    )(*stats, gain, weight, *pieces)


def along(value, axis, step):
    size = 2 if axis in ("core", "z") else 4
    return lax.ppermute(value, axis, [(p, (p + step) % size) for p in range(size)])


def per_device(
    group, pair, mask, ln_gain, ln_shift, w_query, w_key, w_value, w_gate, gate_bias, w_bias,
    w_out, cotangent,
):
    gain, shift = ln_gain.reshape(1, BLOCK), ln_shift.reshape(1, BLOCK)
    half = 2 * group.shape[0]
    bias = bias_call(pair, gain, shift, w_bias.T)
    bias, group, cotangent = lax.optimization_barrier((bias, group, cotangent))
    *sent, coef = project_call(
        group, cotangent, gain, shift, w_query, w_key, w_value, w_gate,
        gate_bias.reshape(1, BLOCK), w_out,
    )
    turned = turn_call([bias] + [along(bias, "zh", d) for d in range(1, 4)])
    pieces = [sent[0]] + [along(sent[d], "y", d) for d in range(1, 4)]
    turned, pieces = lax.optimization_barrier((turned, pieces))
    blocks = [turned[0]] + [along(turned[d], "y", d) for d in range(1, 4)]
    key_value = jnp.stack([p[:half] for p in pieces])
    near = jnp.stack(blocks)
    line, kv_other = lax.optimization_barrier(
        ([near] + [along(near, "x", d) for d in range(1, 4)], along(key_value, "z", 1))
    )
    plane = jnp.stack(line)
    other = along(plane, "core", 1)

    out_own, out_other, out_q, keep, send = attention_call(
        mask.reshape(-1, BLOCK), plane, other, pieces, kv_other
    )

    first = add_core(keep, along(send, "core", 1))
    came = along(out_other, "z", 1)
    sums = [along(first[d], "x", -d) for d in range(1, 4)]
    packed = pack_call(out_own, came, out_q)
    sums, packed = lax.optimization_barrier((sums, packed))
    second = add_four(first[0], *sums)
    back = [packed[0]] + [along(packed[d], "y", -d) for d in range(1, 4)]
    third = [along(second[d], "zh", -d) for d in range(1, 4)]
    third, back = lax.optimization_barrier((third, back))
    last = add_last(second[0], *third)
    last = [last[0]] + [along(last[d], "y", -d) for d in range(1, 4)]

    grad_group = group_call(group, gain, w_query, w_key, w_value, w_gate, coef, back)
    grad_pair = pair_call(pair.shape, stats_call(pair), gain, w_bias.T, last)
    return (grad_group, grad_pair)


def solution(mesh):
    fine = jax.sharding.Mesh(mesh.devices.reshape(4, 4, 2, 2, 4), ("x", "zh", "core", "z", "y"))
    row, col = ("x", "zh", "core"), ("z", "y")
    placed = (
        P(row, col, None),
        P(col, row, None),
        P(), P(), P(), P(), P(), P(), P(), P(), P(), P(),
        P(row, col, None),
    )
    return jax.shard_map(
        per_device,
        mesh=fine,
        in_specs=placed,
        out_specs=(P(row, col, None), P(col, row, None)),
        check_vma=False,
    )
```
